512 devices in a mesh: depth: 32 (over y, x), plane: 16 (over z, core).
Axes of the slice: x: 4, y: 8, z: 8, core: 2. Of those that a mesh axis runs over, the one named last changes fastest.
Arguments:
- activations: bfloat16 [32, 32, 64, 1024], P('plane', 'depth'), may hold values from -6 to 6
- plane_weight: bfloat16 [2, 3, 64, 576], replicated, may hold values from -0.375 to 0.375
- plane_bias: float32 [2, 3, 64], replicated, may hold values from -3 to 3
- depth_weight: bfloat16 [2, 64, 192], replicated, may hold values from -0.75 to 0.75
- depth_bias: float32 [2, 64], replicated, may hold values from -3 to 3
- counts: int32 [16], replicated, may hold values from 1 to 2, as said below
- neighbours: int32 [32, 8], P('plane'), may hold values from -1 to 31, as said below
- voxel_mask: int32 [32, 32, 1024], P('plane', 'depth'), may hold values from 0 to 1, as said below
Outputs:
- hidden: bfloat16 [32, 32, 64, 1024], P('plane', 'depth')
The draws below stay inside these ranges and needn't reach their ends.
Inputs may be any that keep to these rules, and one draw needn't show every extreme that they name: `counts`: each entry is between 1 and 2; at least one entry equals 2. `neighbours`: for a live slot, the live slot that holds the adjacent tile of a grid in that direction, or -1; all -1 for dead slots; neighbourhood is symmetric. `voxel_mask`: zero in dead slots.
All inputs are finite; a program needn't handle non-finite values.
Results may differ from the reference program's by a relative error of at most 0.008.
Values may be sent and summed in bfloat16 or wider, within the bound.
A program may use at most 64 MiB of HBM per device.

```python
import jax
import jax.numpy as jnp
from jax import lax

CHANNELS = 64
TILE = 32
BLOCKS = 2
SLOTS = 2
CELLS = 1024
DEPTH = 32
N_PLANE = 16


def layout(key):
    base_key = jax.random.fold_in(key, 7)
    count_key, owner_key, place_key = jax.random.split(base_key, 3)
    counts = jax.random.randint(count_key, (N_PLANE,), 1, SLOTS + 1)
    full_owner = jax.random.randint(owner_key, (), 0, N_PLANE)
    counts = jnp.where(jnp.arange(N_PLANE) == full_owner, SLOTS, counts).astype(jnp.int32)
    tile_total = N_PLANE * SLOTS
    cell_of = jax.random.permutation(place_key, tile_total)
    cell_tile = jnp.argsort(cell_of, stable=True)
    tile_ids = jnp.arange(tile_total)
    alive = tile_ids % SLOTS < counts[tile_ids // SLOTS]
    grid_row = cell_of // SLOTS
    grid_col = cell_of % SLOTS
    columns = []
    for row_step, col_step in [(-1, -1), (-1, 0), (-1, 1), (0, -1), (0, 1), (1, -1), (1, 0), (1, 1)]:
        new_row = grid_row + row_step
        new_col = grid_col + col_step
        inside = (new_row >= 0) & (new_row < N_PLANE) & (new_col >= 0) & (new_col < SLOTS)
        cell_index = jnp.clip(new_row, 0, N_PLANE - 1) * SLOTS + jnp.clip(new_col, 0, SLOTS - 1)
        other_tile = cell_tile[cell_index]
        linked = inside & alive & alive[other_tile]
        columns.append(jnp.where(linked, other_tile, -1))
    return (counts, jnp.stack(columns, -1).astype(jnp.int32), alive)


def draw_activations(key, part):
    base_key = jax.random.fold_in(key, 23)
    offset_key, noise_key = jax.random.split(base_key, 2)
    tile_total = N_PLANE * SLOTS
    full_shape = (tile_total, DEPTH, CHANNELS, CELLS)
    offsets = jax.random.uniform(offset_key, (tile_total, 1, CHANNELS, 1), jnp.float32, -2.5, 2.5)
    noise = jax.random.normal(noise_key, full_shape, jnp.float32)
    return jnp.clip(offsets + noise, -6.0, 6.0).astype(jnp.bfloat16)


def draw_counts(key, part):
    return layout(key)[0]


def draw_neighbours(key, part):
    return layout(key)[1]


def draw_voxel_mask(key, part):
    alive = layout(key)[2]
    random_bits = jax.random.randint(jax.random.fold_in(key, 11), (N_PLANE * SLOTS, DEPTH, CELLS), 0, 5)
    inside = (random_bits > 0) & alive[:, None, None]
    return jnp.where(inside, 1, 0).astype(jnp.int32)


def normal_values(rng, extent, width, reach, kind=jnp.bfloat16):
    drawn = width * jax.random.normal(rng, extent, jnp.float32)
    return jnp.clip(drawn, min=-reach, max=reach).astype(kind)


def setup_inputs(seed: int = 0) -> dict:
    splits = jax.random.split(jax.random.key(seed), 9)
    return {
        "activations": draw_activations(jax.random.fold_in(splits[8], 71), 0),
        "plane_weight": normal_values(splits[1], (BLOCKS, 3, CHANNELS, 9 * CHANNELS), (4 * CHANNELS) ** -0.5, 0.375),
        "plane_bias": normal_values(splits[2], (BLOCKS, 3, CHANNELS), 0.5, 3.0, jnp.float32),
        "depth_weight": normal_values(splits[3], (BLOCKS, CHANNELS, 3 * CHANNELS), CHANNELS ** -0.5, 0.75),
        "depth_bias": normal_values(splits[4], (BLOCKS, CHANNELS), 0.5, 3.0, jnp.float32),
        "counts": draw_counts(jax.random.fold_in(splits[8], 71), 0),
        "neighbours": draw_neighbours(jax.random.fold_in(splits[8], 71), 0),
        "voxel_mask": draw_voxel_mask(jax.random.fold_in(splits[8], 71), 0),
    }


def flatten(array):
    return array.reshape(array.shape[:-2] + (-1,))


def strips(tile_view, strip_width):
    top_rows = tile_view[..., :strip_width, :]
    bottom = tile_view[..., TILE - strip_width:, :]
    left_cols = tile_view[..., :, :strip_width]
    right_cols = tile_view[..., :, TILE - strip_width:]
    return jnp.concatenate([flatten(top_rows), flatten(bottom), flatten(left_cols), flatten(right_cols)], -1)


def surround(center, neighbour_table, strip_pool, strip_width):
    length = strip_width * TILE
    present = neighbour_table >= 0
    safe_index = jnp.maximum(neighbour_table, 0)

    def fetch_strip(column, segment, piece_shape):
        pieces = strip_pool[safe_index[:, column]][..., segment * length:(segment + 1) * length]
        pieces = pieces.reshape(pieces.shape[:-1] + piece_shape)
        keep = present[:, column].reshape((-1,) + (1,) * (pieces.ndim - 1))
        return jnp.where(keep, pieces, jnp.zeros_like(pieces))

    rows_shape = (strip_width, TILE)
    cols_shape = (TILE, strip_width)
    north_west = fetch_strip(0, 1, rows_shape)[..., TILE - strip_width:]
    north = fetch_strip(1, 1, rows_shape)
    north_east = fetch_strip(2, 1, rows_shape)[..., :strip_width]
    west_side = fetch_strip(3, 3, cols_shape)
    east_side = fetch_strip(4, 2, cols_shape)
    south_west = fetch_strip(5, 0, rows_shape)[..., TILE - strip_width:]
    south_side = fetch_strip(6, 0, rows_shape)
    south_east = fetch_strip(7, 0, rows_shape)[..., :strip_width]
    upper_band = jnp.concatenate([north_west, north, north_east], -1)
    middle = jnp.concatenate([west_side, center, east_side], -1)
    lower_band = jnp.concatenate([south_west, south_side, south_east], -1)
    return jnp.concatenate([upper_band, middle, lower_band], -2)


def plane_conv(padded, weight):
    inner = padded.shape[-1] - 2
    tap_list = [padded[..., row_off:row_off + inner, col_off:col_off + inner] for row_off in range(3) for col_off in range(3)]
    stacked = jnp.concatenate(tap_list, axis=-3)
    stacked = stacked.reshape(stacked.shape[:-2] + (inner * inner,))
    return jnp.einsum("ok,nskq->nsoq", weight.astype(jnp.float32), stacked.astype(jnp.float32))


def reference(activations, plane_weight, plane_bias, depth_weight, depth_bias, counts, neighbours, voxel_mask):
    tile_ids = jnp.arange(N_PLANE * SLOTS, dtype=jnp.int32)
    alive = (tile_ids % SLOTS) < counts[tile_ids // SLOTS]
    hidden = jnp.where(alive[:, None, None, None], activations, jnp.zeros_like(activations))
    mask_f = voxel_mask.astype(jnp.float32)[:, :, None, :]
    grouped_table = neighbours.reshape(N_PLANE, SLOTS, 8)
    grouped_mask = mask_f.reshape(N_PLANE, SLOTS, DEPTH, 1, CELLS)
    full_shape = hidden.shape
    for block_id in range(BLOCKS):
        branch = hidden
        for layer_id in range(3):
            strip_pool = strips(branch.reshape(full_shape[:-1] + (TILE, TILE)), 1)
            weight = plane_weight[block_id, layer_id]
            offsets = plane_bias[block_id, layer_id][:, None]

            def layer_group(operands):
                group_tiles, group_table, group_mask = operands
                padded = surround(group_tiles.reshape(group_tiles.shape[:-1] + (TILE, TILE)), group_table, strip_pool, 1)
                summed = plane_conv(padded, weight)
                return (group_mask * jax.nn.silu(summed + offsets)).astype(jnp.bfloat16)

            branch = lax.map(layer_group, (branch.reshape((N_PLANE, SLOTS) + full_shape[1:]), grouped_table, grouped_mask)).reshape(full_shape)
        padded_z = jnp.pad(branch, ((0, 0), (1, 1), (0, 0), (0, 0)))
        weight_d = depth_weight[block_id].astype(jnp.float32)
        offsets_d = depth_bias[block_id][:, None]

        def depth_group(operands):
            group_pad, group_mask, group_hidden = operands
            stacked = jnp.concatenate([group_pad[:, :-2], group_pad[:, 1:-1], group_pad[:, 2:]], axis=2)
            summed = jnp.einsum("ok,nskq->nsoq", weight_d, stacked.astype(jnp.float32))
            return (group_hidden.astype(jnp.float32) + group_mask * (summed + offsets_d)).astype(jnp.bfloat16)

        hidden = lax.map(depth_group, (padded_z.reshape((N_PLANE, SLOTS) + padded_z.shape[1:]), grouped_mask, hidden.reshape((N_PLANE, SLOTS) + full_shape[1:]))).reshape(full_shape)
    return hidden
```

```python
import functools

import jax
import jax.numpy as jnp
from jax import lax
from jax.experimental import pallas as pl
from jax.experimental.pallas import tpu as pltpu
from jax.sharding import PartitionSpec as P


F32, BF16 = jnp.float32, jnp.bfloat16
MESH = pl.DeviceIdType.MESH
RIGHT, LEFT = 0, 1
NW, N, NE, W, E, SW, S, SE = range(8)
TOP, BOTTOM, ROWS2, FIRST, LAST, COLS2 = range(6)


def iota(shape, dim):
    return lax.broadcasted_iota(jnp.int32, shape, dim)


def turn(x, k):
    k %= 16
    return pltpu.roll(x, k, 0) if k else x


def dot(a, b, ca=1, cb=0):
    return lax.dot_general(a, b, (((ca,), (cb,)), ((), ())), preferred_element_type=F32)


def row_strip(slab, a):
    row = iota((16, 1), 0)
    out = turn(slab(0), -4 * a)
    for j in range(1, 4):
        out = jnp.where(row // 4 == j, turn(slab(j), 4 * j - 4 * a), out)
    return out


def col_strip(slab, b):
    row = iota((16, 1), 0)
    out = turn(slab(0), -b)
    for i in range(1, 4):
        out = jnp.where(row % 4 == i, turn(slab(i), i - b), out)
    return out


def strip_halves(slab, wide):
    low = iota((16, 128), 1) < 64
    out = {}
    for half in range(2):
        out[TOP, half] = row_strip(lambda j: slab(0, j, half), 0)
        out[BOTTOM, half] = row_strip(lambda j: slab(3, j, half), 3)
        out[FIRST, half] = col_strip(lambda i: slab(i, 0, half), 0)
        out[LAST, half] = col_strip(lambda i: slab(i, 3, half), 3)
        if wide:
            if half == 0:
                out[ROWS2, half] = row_strip(lambda j: slab(1, j, half), 0)
            else:
                out[ROWS2, half] = row_strip(lambda j: slab(2, j, half), 3)
            out[COLS2, half] = jnp.where(
                low, col_strip(lambda i: slab(i, 1, half), 0), col_strip(lambda i: slab(i, 2, half), 3)
            )
    return out


def surround(slab, strip, width, emit):
    row = iota((16, 1), 0)
    first, last = row % 4 == 0, row % 4 == 3
    top, bottom = row < 4, row >= 12
    cols = range(-width, 4 + width)
    for half in range(2):

        def widened(i):
            out = {j: slab(i, j, half) for j in range(4)}
            for j in cols:
                if j == -1:
                    out[j] = jnp.where(first, turn(strip(W, LAST, half), -i), turn(slab(i, 3, half), 1))
                if j == -2:
                    out[j] = jnp.where(first, turn(strip(W, COLS2, half), -i), turn(slab(i, 2, half), 1))
                if j == 4:
                    out[j] = jnp.where(last, turn(strip(E, FIRST, half), 3 - i), turn(slab(i, 0, half), -1))
                if j == 5:
                    out[j] = jnp.where(last, turn(strip(E, COLS2, half), 3 - i), turn(slab(i, 1, half), -1))
            return out

        def beyond(kind, mid, before, after, base, j):
            own = strip(mid, kind, half)
            if 0 <= j < 4:
                return turn(own, base - 4 * j)
            if j == -1:
                return jnp.where(first, turn(strip(before, kind, half), base + 1), turn(own, base - 11))
            if j == -2:
                return jnp.where(first, turn(strip(before, kind, half), base - 11), turn(own, base - 7))
            if j == 4:
                return jnp.where(last, turn(strip(after, kind, half), base + 3), turn(own, base - 1))
            return jnp.where(last, turn(strip(after, kind, half), base - 1), turn(own, base - 5))

        for i in range(4):
            line = widened(i)
            emit(i, half, [line[j] for j in cols])
            if i == 0:
                emit(4, half, [
                    jnp.where(bottom, beyond(TOP, S, SW, SE, 12, j), turn(line[j], -4)) for j in cols
                ])
            if i == 1 and width == 2 and half == 0:
                emit(5, half, [
                    jnp.where(bottom, beyond(ROWS2, S, SW, SE, 12, j), turn(line[j], -4)) for j in cols
                ])
            if i == 2 and width == 2 and half == 1:
                emit(-2, half, [
                    jnp.where(top, beyond(ROWS2, N, NW, NE, 0, j), turn(line[j], 4)) for j in cols
                ])
            if i == 3:
                emit(-1, half, [
                    jnp.where(top, beyond(BOTTOM, N, NW, NE, 0, j), turn(line[j], 4)) for j in cols
                ])


def emit_odd(store, width, side):
    def emit(row, half, slabs):
        low = iota((16, 128), 1) < 64
        i = row + width - (1 - half)
        if 0 <= i < side:
            for j in range(side):
                store(i, j, half, jnp.where(low, slabs[j + 1], slabs[j]))

    return emit


def body(
    n_depth, n_plane,
    act, pw, pb, dw, db, cnt, nbr, vm, out,
    sel, hid, msk, x_in, y1, y2, branch, m1, m2, weights, dweights,
    pool0, pool1, mpool, rim, rim_in, rim_mask, full_in,
    ring_ss, ring_rs, sib_ss, sib_rs, rim_ss, rim_rs, full_ss, full_rs,
):
    n_z = n_plane // 2
    half_z = n_z // 2
    pools = (pool0, pool1)
    d = lax.axis_index("depth")
    p = lax.axis_index("plane")
    z, c = p // 2, p % 2

    def z_at(offset):
        return lax.rem(z + offset + n_z, n_z)

    def plane_id(offset, core):
        return z_at(offset) * 2 + core

    def depth_id(way):
        return lax.rem(d + (1 if way == 0 else n_depth - 1), n_depth)

    barrier = pltpu.get_barrier_semaphore()
    for target in (
        {"plane": plane_id(1, c)}, {"plane": plane_id(-1, c)}, {"plane": z * 2 + 1 - c},
        {"depth": depth_id(0)}, {"depth": depth_id(1)},
    ):
        pl.semaphore_signal(barrier, inc=1, device_id=target, device_id_type=MESH)

    def block_ref(g, owner, item):
        return mpool.at[owner] if item == 2 else pools[g].at[2 * owner + item]

    def ring_copy(g, way, step, item, owner_offset):
        ref = block_ref(g, plane_id(owner_offset, c), item)
        return pltpu.make_async_remote_copy(
            src_ref=ref, dst_ref=ref, send_sem=ring_ss.at[g, way, step, item], recv_sem=ring_rs.at[g, way, step, item],
            device_id={"plane": plane_id(1 if way == RIGHT else -1, c)}, device_id_type=MESH,
        )

    def ring_out(g, way, step, item):
        return ring_copy(g, way, step, item, -step if way == RIGHT else step)

    def ring_in(g, way, step, item):
        return ring_copy(g, way, step, item, -step - 1 if way == RIGHT else step + 1)

    def sib_copy(g, way, step, item, core):
        owner = plane_id(-step - 1 if way == RIGHT else step + 1, core)
        key = 0 if step < 0 else 1 + way * half_z + step
        ref = block_ref(g, owner, item)
        return pltpu.make_async_remote_copy(
            src_ref=ref, dst_ref=ref, send_sem=sib_ss.at[g, key, item], recv_sem=sib_rs.at[g, key, item],
            device_id={"plane": z * 2 + 1 - c}, device_id_type=MESH,
        )

    def items(g, way, step):
        if step < half_z - 1:
            got = (0, 1)
        else:
            got = (0,) if way == RIGHT else (1,)
        if g == 0 and (step < half_z - 1 or way == RIGHT):
            got += (2,)
        return got

    def launch(g, item):
        for way in (RIGHT, LEFT):
            if item in items(g, way, 0):
                ring_out(g, way, 0, item).start()
        sib_copy(g, RIGHT, -1, item, c).start()

    def pass_on(g, step):
        for item in range(3):
            for way in (RIGHT, LEFT):
                if item in items(g, way, step):
                    ring_in(g, way, step, item).wait_recv()
                    if step + 1 < half_z and item in items(g, way, step + 1):
                        ring_out(g, way, step + 1, item).start()
                    sib_copy(g, way, step, item, c).start()

    def all_steps(g):
        got = [(RIGHT, -1, item) for item in ((0, 1, 2) if g == 0 else (0, 1))]
        for step in range(half_z):
            for way in (RIGHT, LEFT):
                got += [(way, step, item) for item in items(g, way, step)]
        return got

    def collect(g):
        for way, step, item in all_steps(g):
            sib_copy(g, way, step, item, 1 - c).wait_recv()

    def settle(g):
        for way, step, item in all_steps(g):
            sib_copy(g, way, step, item, c).wait_send()
            if step >= 0:
                ring_out(g, way, step, item).wait_send()

    def rim_copy(way, t):
        return pltpu.make_async_remote_copy(
            src_ref=rim.at[t], dst_ref=rim_in.at[way, t], send_sem=rim_ss.at[way, t], recv_sem=rim_rs.at[way, t],
            device_id={"depth": depth_id(way)}, device_id_type=MESH,
        )

    def full_copy(blk, way, t):
        return pltpu.make_async_remote_copy(
            src_ref=branch.at[blk, t], dst_ref=full_in.at[blk, way, t],
            send_sem=full_ss.at[blk, way, t], recv_sem=full_rs.at[blk, way, t],
            device_id={"depth": depth_id(way)}, device_id_type=MESH,
        )

    r = iota((512, 1), 0)
    q, i, j, a, b = r // 128, (r // 32) % 4, (r // 8) % 4, (r // 4) % 2, r % 4
    cell = a * 256 + i * 64 + (q // 2) * 32 + b * 8 + j * 2 + q % 2
    sel[...] = jnp.where(cell == iota((512, 512), 1), 1.0, 0.0).astype(BF16)

    low128 = iota((128, 128), 1) < 64
    low16 = iota((16, 128), 1) < 64
    low64 = iota((64, 128), 1) < 64

    def to_patches(src, dst, live):
        for h in range(2):
            v = dot(sel[...], src[:, h * 512 : (h + 1) * 512], 1, 1)
            v = jnp.where(live > slot, v, 0.0)
            for half in range(2):
                even, odd = (v[(2 * half + k) * 128 : (2 * half + k + 1) * 128] for k in range(2))
                lanes = slice(half * 128, half * 128 + 128)
                rows = slice(h * 8, h * 8 + 8)
                dst[0, :, rows, lanes] = jnp.where(low128, even, pltpu.roll(odd, 64, 1)).reshape(16, 8, 128)
                dst[1, :, rows, lanes] = jnp.where(low128, pltpu.roll(even, 64, 1), odd).reshape(16, 8, 128)

    slot = iota((1, 128), 1) // 64
    to_patches(act[...], hid, cnt[p])

    def half_of(half):
        return slice(half * 128, half * 128 + 128)

    def slab_of(ref, t):
        return lambda i, j, half: ref[t, 4 * i + j, :, half_of(half)]

    for t in range(2):
        for (kind, half), value in strip_halves(slab_of(hid, t), True).items():
            pool0[2 * p + t, kind, :, half_of(half)] = value.astype(BF16)

    pl.semaphore_wait(barrier, 5)
    launch(0, 0)
    launch(0, 1)

    spread = jnp.concatenate(
        [jnp.broadcast_to(vm[t].astype(F32), (64, 1024)) for t in range(2)], axis=0
    ).astype(BF16)
    to_patches(spread, msk, 2)
    lane64 = iota((16, 128), 1) % 64
    mask_out = jnp.zeros((16, 128), F32)
    for t in range(2):
        strips = strip_halves(slab_of(msk, t), True)
        for (kind, half), value in strips.items():
            rim_mask[t, kind, :, half_of(half)] = value
            if kind in (TOP, BOTTOM, FIRST, LAST):
                order = (TOP, BOTTOM, FIRST, LAST).index(kind)
                mask_out = jnp.where(lane64 == half * 8 + t * 4 + order, value, mask_out)
    mpool[p] = mask_out.astype(BF16)
    launch(0, 2)

    def twice(w):
        unit = jnp.where(iota((64, 128), 0) == iota((64, 128), 1) % 64, 1.0, 0.0).astype(BF16)
        return dot(w, unit, 0, 0)

    def plane_weights(blk, layer):
        w = twice(pw[blk, layer])
        mirror_in, mirror_out = layer != 1, layer == 1
        for s in range(4):
            for q in range(4):
                u = 2 * (s // 2) + (1 - q // 2 if mirror_in else q // 2)
                v = 2 * (s % 2) + (1 - q % 2 if mirror_in else q % 2)
                rows = slice((s * 4 + q) * 64, (s * 4 + q + 1) * 64)
                for half in range(2):
                    parts = []
                    for col in range(2):
                        dr = u - (1 - half if mirror_out else half)
                        dc = v - (1 - col if mirror_out else col)
                        ok = 0 <= dr < 3 and 0 <= dc < 3
                        tap = dr * 3 + dc
                        parts.append(w[tap * 64 : (tap + 1) * 64] if ok else jnp.zeros((64, 128), F32))
                    weights[blk * 3 + layer, rows, half_of(half)] = jnp.where(low64, *parts).astype(BF16)

    def depth_weights(blk):
        w = twice(dw[blk])
        zero = jnp.zeros((64, 128), F32)
        for tap in range(3):
            part = w[tap * 64 : (tap + 1) * 64]
            if tap == 0:
                part = jnp.where(d > 0, part, 0.0)
            if tap == 2:
                part = jnp.where(d < n_depth - 1, part, 0.0)
            for q in range(4):
                rows = slice(tap * 256 + q * 64, tap * 256 + (q + 1) * 64)
                mine = jnp.where(low64, part, 0.0) if q % 2 == 0 else jnp.where(low64, 0.0, part)
                for half in range(2):
                    dweights[blk, rows, half_of(half)] = (mine if q // 2 == half else zero).astype(BF16)

    def four(v):
        two = jnp.concatenate([v, v], axis=1)
        return jnp.concatenate([two, two], axis=1)

    plane_weights(0, 0)
    pass_on(0, 0)
    plane_weights(0, 1)
    for step in range(1, half_z):
        pass_on(0, step)
        if step == 1:
            plane_weights(0, 2)
            depth_weights(0)
    collect(0)

    group = {NW: BOTTOM, N: BOTTOM, NE: BOTTOM, W: LAST, E: FIRST, SW: TOP, S: TOP, SE: TOP}

    def around_mask(t, carry):
        spot = iota((16, 128), 1) % 64
        found = {}
        for kind in (TOP, BOTTOM, FIRST, LAST):
            order = (TOP, BOTTOM, FIRST, LAST).index(kind)
            ways = [k for k in range(8) if group[k] == kind]
            rows = []
            for k in ways:
                other = nbr[t, k]
                at = jnp.maximum(other, 0)
                keep = (spot % 8) // 4 == jnp.where(other >= 0, at % 2, 2)
                rows.append(jnp.where(keep, mpool[at // 2].astype(F32), 0.0))
            m, n = iota((128, 256), 0), iota((128, 256), 1)
            hit = (m // 64 == (n % 128) // 64) & ((m % 64) // 8 == n // 128) & (m % 4 == order)
            wide = dot(jnp.concatenate(rows, axis=0).astype(BF16), jnp.where(hit, 1.0, 0.0).astype(BF16))
            for at, k in enumerate(ways):
                found[k] = wide[at * 16 : at * 16 + 16]

        def store_odd(i, j, half, value):
            m2[t, i, j, :, half_of(half)] = value

        odd = emit_odd(store_odd, 1, 5)

        def emit(row, half, slabs):
            for j in range(6):
                m1[t, row + 1, j, :, half_of(half)] = slabs[j]
            odd(row, half, slabs)

        surround(slab_of(msk, t), lambda k, kind, half: found[k][:, half_of(half)], 1, emit)
        return carry

    lax.fori_loop(0, 2, around_mask, 0)

    def conv(blk, layer, src, side, mask, store):
        cells = (side - 1) ** 2
        taps = [
            src[si : si + side - 1, sj : sj + side - 1].reshape(cells * 16, 256)
            for si in range(2)
            for sj in range(2)
        ]
        total = dot(jnp.concatenate(taps, axis=1), weights[blk * 3 + layer])
        total = total + four(pb[blk, layer : layer + 1, :])
        gated = total * (0.5 + 0.5 * jnp.tanh(0.5 * total))
        store((gated * mask.reshape(cells * 16, 256)).astype(BF16))

    def plane_layers(blk):
        def tile(t, carry):
            def store_odd(i, j, half, value):
                x_in[i, j, :, half_of(half)] = value.astype(BF16)

            def strip(k, kind, half):
                other = nbr[t, k]
                value = pools[blk][jnp.maximum(other, 0), kind, :, half_of(half)].astype(F32)
                return jnp.where(other >= 0, value, 0.0)

            surround(slab_of(hid, t), strip, 2, emit_odd(store_odd, 2, 7))

            def to_y1(value):
                y1[...] = value.reshape(6, 6, 16, 256)

            def to_y2(value):
                y2[...] = value.reshape(5, 5, 16, 256)

            def to_branch(value):
                branch[blk, t] = value.reshape(16, 16, 256)

            conv(blk, 0, x_in, 7, m1[t], to_y1)
            conv(blk, 1, y1, 6, m2[t], to_y2)
            conv(blk, 2, y2, 5, msk[t], to_branch)
            if blk == 0:
                slab = lambda i, j, half: branch[0, t, 4 * i + j, :, half_of(half)].astype(F32)
                for (kind, half), value in strip_halves(slab, True).items():
                    rim[t, kind, :, half_of(half)] = value.astype(BF16)
                for way in range(2):
                    rim_copy(way, t).start()
            else:
                for way in range(2):
                    full_copy(1, way, t).start()
            return carry

        lax.fori_loop(0, 2, tile, 0)

    def along_depth(blk, below, own, above):
        return dot(jnp.concatenate([below, own, above], axis=1), dweights[blk]) + four(db[blk : blk + 1, :])

    def residual(blk, t):
        for way in range(2):
            full_copy(blk, way, t).wait_recv()
        total = along_depth(
            blk, full_in[blk, 0, t].reshape(256, 256), branch[blk, t].reshape(256, 256),
            full_in[blk, 1, t].reshape(256, 256),
        )
        new = hid[t].reshape(256, 256) + msk[t].reshape(256, 256) * total
        hid[t] = new.astype(BF16).astype(F32).reshape(16, 16, 256)

    plane_layers(0)
    for t in range(2):
        for way in range(2):
            full_copy(0, way, t).start()
    for t in range(2):
        for way in range(2):
            rim_copy(way, t).wait_recv()
        total = along_depth(
            0, rim_in[0, t].reshape(96, 256), rim[t].reshape(96, 256), rim_in[1, t].reshape(96, 256)
        )
        old = pool0[2 * p + t].astype(F32).reshape(96, 256)
        new = old + rim_mask[t].reshape(96, 256) * total
        pool1[2 * p + t] = new.astype(BF16).reshape(6, 16, 256)
        launch(1, t)
    plane_weights(1, 0)
    pass_on(1, 0)
    plane_weights(1, 1)
    for step in range(1, half_z):
        pass_on(1, step)
        if step == 1:
            plane_weights(1, 2)
            depth_weights(1)
        if step == max(half_z - 2, 1):
            for t in range(2):
                residual(0, t)
    collect(1)
    plane_layers(1)
    for t in range(2):
        residual(1, t)

    for h in range(2):
        parts = []
        for half in range(2):
            lanes, rows = half_of(half), slice(h * 8, h * 8 + 8)
            one = hid[0, :, rows, lanes].reshape(128, 128)
            two = hid[1, :, rows, lanes].reshape(128, 128)
            parts.append(jnp.where(low128, one, pltpu.roll(two, 64, 1)))
            parts.append(jnp.where(low128, pltpu.roll(one, 64, 1), two))
        back = dot(jnp.concatenate(parts, axis=0).astype(BF16), sel[...], 0, 0)
        out[:, h * 512 : (h + 1) * 512] = back.astype(BF16)

    settle(0)
    settle(1)
    for t in range(2):
        for way in range(2):
            rim_copy(way, t).wait_send()
            for blk in range(2):
                full_copy(blk, way, t).wait_send()


def shards(mesh, activations, plane_weight, plane_bias, depth_weight, depth_bias, counts, neighbours, voxel_mask):
    n_depth, n_plane = mesh.shape["depth"], mesh.shape["plane"]
    half_z = n_plane // 4
    vmem = pl.BlockSpec(memory_space=pltpu.VMEM)
    smem = pl.BlockSpec(memory_space=pltpu.SMEM)
    dma = pltpu.SemaphoreType.DMA
    out = pl.pallas_call(
        functools.partial(body, n_depth, n_plane),
        out_shape=jax.ShapeDtypeStruct((128, 1024), BF16),
        in_specs=[vmem] * 5 + [smem, smem, vmem],
        out_specs=vmem,
        scratch_shapes=[
            pltpu.VMEM((512, 512), BF16),
            pltpu.VMEM((2, 16, 16, 256), F32),
            pltpu.VMEM((2, 16, 16, 256), F32),
            pltpu.VMEM((7, 7, 16, 256), BF16),
            pltpu.VMEM((6, 6, 16, 256), BF16),
            pltpu.VMEM((5, 5, 16, 256), BF16),
            pltpu.VMEM((2, 2, 16, 16, 256), BF16),
            pltpu.VMEM((2, 6, 6, 16, 256), F32),
            pltpu.VMEM((2, 5, 5, 16, 256), F32),
            pltpu.VMEM((6, 1024, 256), BF16),
            pltpu.VMEM((2, 768, 256), BF16),
            pltpu.VMEM((2 * n_plane, 6, 16, 256), BF16),
            pltpu.VMEM((2 * n_plane, 6, 16, 256), BF16),
            pltpu.VMEM((n_plane, 16, 128), BF16),
            pltpu.VMEM((2, 6, 16, 256), BF16),
            pltpu.VMEM((2, 2, 6, 16, 256), BF16),
            pltpu.VMEM((2, 6, 16, 256), F32),
            pltpu.VMEM((2, 2, 2, 16, 16, 256), BF16),
            dma((2, 2, half_z, 3)),
            dma((2, 2, half_z, 3)),
            dma((2, 1 + 2 * half_z, 3)),
            dma((2, 1 + 2 * half_z, 3)),
            dma((2, 2)),
            dma((2, 2)),
            dma((2, 2, 2)),
            dma((2, 2, 2)),
        ],
        compiler_params=pltpu.CompilerParams(
            collective_id=0, has_side_effects=True, vmem_limit_bytes=56 * 2**20
        ),
    )(
        activations.reshape(128, 1024), plane_weight, plane_bias, depth_weight, depth_bias, counts, neighbours,
        voxel_mask,
    )
    return out.reshape(activations.shape)


def solution(mesh):
    in_specs = (
        P("plane", "depth", None, None),
        P(),
        P(),
        P(),
        P(),
        P(),
        P("plane", None),
        P("plane", "depth", None),
    )
    out_specs = P("plane", "depth", None, None)
    return jax.shard_map(
        functools.partial(shards, mesh), mesh=mesh, in_specs=in_specs, out_specs=out_specs, check_vma=False
    )
```

```python
import functools

import jax
import jax.numpy as jnp
from jax import lax
from jax.experimental import pallas as pl
from jax.experimental.pallas import tpu as pltpu
from jax.sharding import PartitionSpec as P


F32, BF16 = jnp.float32, jnp.bfloat16
MESH = pl.DeviceIdType.MESH
RIGHT, LEFT = 0, 1
MASK = 2
NW, N, NE, W, E, SW, S, SE = range(8)
TOP, BOTTOM, ROWS2, FIRST, LAST, COLS2 = range(6)


def iota(shape, dim):
    return lax.broadcasted_iota(jnp.int32, shape, dim)


def turn(x, k):
    k %= 16
    return pltpu.roll(x, k, 0) if k else x


def dot(a, b, ca=1, cb=0):
    return lax.dot_general(a, b, (((ca,), (cb,)), ((), ())), preferred_element_type=F32)


def row_strip(slab, a):
    row = iota((16, 1), 0)
    out = turn(slab(0), -4 * a)
    for j in range(1, 4):
        out = jnp.where(row // 4 == j, turn(slab(j), 4 * j - 4 * a), out)
    return out


def col_strip(slab, b):
    row = iota((16, 1), 0)
    out = turn(slab(0), -b)
    for i in range(1, 4):
        out = jnp.where(row % 4 == i, turn(slab(i), i - b), out)
    return out


def strip_halves(slab, wide):
    low = iota((16, 128), 1) < 64
    out = {}
    for half in range(2):
        out[TOP, half] = row_strip(lambda j: slab(0, j, half), 0)
        out[BOTTOM, half] = row_strip(lambda j: slab(3, j, half), 3)
        out[FIRST, half] = col_strip(lambda i: slab(i, 0, half), 0)
        out[LAST, half] = col_strip(lambda i: slab(i, 3, half), 3)
        if wide:
            if half == 0:
                out[ROWS2, half] = row_strip(lambda j: slab(1, j, half), 0)
            else:
                out[ROWS2, half] = row_strip(lambda j: slab(2, j, half), 3)
            out[COLS2, half] = jnp.where(
                low, col_strip(lambda i: slab(i, 1, half), 0), col_strip(lambda i: slab(i, 2, half), 3)
            )
    return out


def surround(slab, strip, width, emit):
    row = iota((16, 1), 0)
    first, last = row % 4 == 0, row % 4 == 3
    top, bottom = row < 4, row >= 12
    cols = range(-width, 4 + width)
    for half in range(2):

        def widened(i):
            out = {j: slab(i, j, half) for j in range(4)}
            for j in cols:
                if j == -1:
                    out[j] = jnp.where(first, turn(strip(W, LAST, half), -i), turn(slab(i, 3, half), 1))
                if j == -2:
                    out[j] = jnp.where(first, turn(strip(W, COLS2, half), -i), turn(slab(i, 2, half), 1))
                if j == 4:
                    out[j] = jnp.where(last, turn(strip(E, FIRST, half), 3 - i), turn(slab(i, 0, half), -1))
                if j == 5:
                    out[j] = jnp.where(last, turn(strip(E, COLS2, half), 3 - i), turn(slab(i, 1, half), -1))
            return out

        def beyond(kind, mid, before, after, base, j):
            own = strip(mid, kind, half)
            if 0 <= j < 4:
                return turn(own, base - 4 * j)
            if j == -1:
                return jnp.where(first, turn(strip(before, kind, half), base + 1), turn(own, base - 11))
            if j == -2:
                return jnp.where(first, turn(strip(before, kind, half), base - 11), turn(own, base - 7))
            if j == 4:
                return jnp.where(last, turn(strip(after, kind, half), base + 3), turn(own, base - 1))
            return jnp.where(last, turn(strip(after, kind, half), base - 1), turn(own, base - 5))

        for i in range(4):
            line = widened(i)
            emit(i, half, [line[j] for j in cols])
            if i == 0:
                emit(4, half, [
                    jnp.where(bottom, beyond(TOP, S, SW, SE, 12, j), turn(line[j], -4)) for j in cols
                ])
            if i == 1 and width == 2 and half == 0:
                emit(5, half, [
                    jnp.where(bottom, beyond(ROWS2, S, SW, SE, 12, j), turn(line[j], -4)) for j in cols
                ])
            if i == 2 and width == 2 and half == 1:
                emit(-2, half, [
                    jnp.where(top, beyond(ROWS2, N, NW, NE, 0, j), turn(line[j], 4)) for j in cols
                ])
            if i == 3:
                emit(-1, half, [
                    jnp.where(top, beyond(BOTTOM, N, NW, NE, 0, j), turn(line[j], 4)) for j in cols
                ])


def emit_odd(store, width, side):
    def emit(row, half, slabs):
        low = iota((16, 128), 1) < 64
        i = row + width - (1 - half)
        if 0 <= i < side:
            for j in range(side):
                store(i, j, half, jnp.where(low, slabs[j + 1], slabs[j]))

    return emit


def body(
    n_depth, n_plane,
    act, pw, pb, dw, db, cnt, nbr, vm, out,
    sel, hid, msk, x_in, y1, y2, y3, branch, m1, m2, weights, dweights,
    pool0, pool1, mpool, rim, rim_in, rim_mask, full_in,
    ring_ss, ring_rs, sib_ss, sib_rs, rim_ss, rim_rs, full_ss, full_rs,
):
    n_z = n_plane // 2
    pools = (pool0, pool1)
    d = lax.axis_index("depth")
    p = lax.axis_index("plane")
    z, c = p // 2, p % 2

    def z_at(offset):
        return lax.rem(z + offset + n_z, n_z)

    def plane_id(offset, core):
        return z_at(offset) * 2 + core

    def depth_id(way):
        return lax.rem(d + (1 if way == 0 else n_depth - 1), n_depth)

    barrier = pltpu.get_barrier_semaphore()
    for target in (
        {"plane": plane_id(1, c)}, {"plane": plane_id(-1, c)}, {"plane": z * 2 + 1 - c},
        {"plane": plane_id(2, c)}, {"plane": plane_id(-2, c)},
        {"depth": depth_id(0)}, {"depth": depth_id(1)},
    ):
        pl.semaphore_signal(barrier, inc=1, device_id=target, device_id_type=MESH)

    def block_ref(g, owner, item):
        return mpool.at[owner] if item == MASK else pools[g].at[2 * owner + item]

    def ring_copy(g, way, k, m, item, owner_at):
        sign = -1 if way == RIGHT else 1
        ref = block_ref(g, plane_id(sign * owner_at, c), item)
        return pltpu.make_async_remote_copy(
            src_ref=ref, dst_ref=ref, send_sem=ring_ss.at[g, way, k + m - 1, item],
            recv_sem=ring_rs.at[g, way, k + m - 1, item],
            device_id={"plane": plane_id(-sign * m, c)}, device_id_type=MESH,
        )

    def ring_out(g, way, k, m, item):
        return ring_copy(g, way, k, m, item, k)

    def ring_in(g, way, dist, item):
        return ring_copy(g, way, dist - 1, 1, item, dist)

    def sib_copy(g, way, dist, item, core):
        owner = plane_id(-dist if way == RIGHT else dist, core)
        key = 0 if dist == 0 else way * 4 + dist
        ref = block_ref(g, owner, item)
        return pltpu.make_async_remote_copy(
            src_ref=ref, dst_ref=ref, send_sem=sib_ss.at[g, key, item], recv_sem=sib_rs.at[g, key, item],
            device_id={"plane": z * 2 + 1 - c}, device_id_type=MESH,
        )

    def leads(way):
        return 0 if way == RIGHT else 1

    def items(g, way, dist):
        got = (leads(way), 1 - leads(way))
        if dist == 4:
            got = got[:1]
        if g == 0 and (dist < 4 or way == RIGHT):
            got += (MASK,)
        return got

    def onward(g, way, dist, item):
        got = []
        if dist == 2 and item in items(g, way, 4):
            got.append(ring_out(g, way, 2, 2, item))
        if dist < 3:
            got.append(ring_out(g, way, dist, 1, item))
        return got

    def launch(g, way, item):
        for copy in onward(g, way, 0, item):
            copy.start()

    def share(g, item):
        sib_copy(g, RIGHT, 0, item, c).start()

    def pass_on(g, *dists):
        order = sorted(
            (items(g, way, dist).index(item) * 2 if item != MASK else 9, dist, way, item)
            for dist in dists for way in (RIGHT, LEFT) for item in items(g, way, dist)
        )
        for _, dist, way, item in order:
            ring_in(g, way, dist, item).wait_recv()
            for copy in onward(g, way, dist, item):
                copy.start()
            sib_copy(g, way, dist, item, c).start()

    def everything(g):
        got = [(RIGHT, 0, item) for item in ((0, 1, MASK) if g == 0 else (0, 1))]
        return got + [(way, dist, item) for dist in range(1, 5) for way in (RIGHT, LEFT) for item in items(g, way, dist)]

    def collect(g):
        for way, dist, item in everything(g):
            sib_copy(g, way, dist, item, 1 - c).wait_recv()

    def settle(g):
        for way, dist, item in everything(g):
            sib_copy(g, way, dist, item, c).wait_send()
        for dist in range(3):
            for way in (RIGHT, LEFT):
                for item in items(g, way, max(dist, 1)):
                    for copy in onward(g, way, dist, item):
                        copy.wait_send()

    def rim_copy(blk, way, t):
        return pltpu.make_async_remote_copy(
            src_ref=rim.at[blk, t], dst_ref=rim_in.at[blk, way, t],
            send_sem=rim_ss.at[blk, way, t], recv_sem=rim_rs.at[blk, way, t],
            device_id={"depth": depth_id(way)}, device_id_type=MESH,
        )

    def full_copy(blk, way, t):
        return pltpu.make_async_remote_copy(
            src_ref=branch.at[blk, t], dst_ref=full_in.at[blk, way, t],
            send_sem=full_ss.at[blk, way, t], recv_sem=full_rs.at[blk, way, t],
            device_id={"depth": depth_id(way)}, device_id_type=MESH,
        )

    r = iota((512, 1), 0)
    q, i, j, a, b = r // 128, (r // 32) % 4, (r // 8) % 4, (r // 4) % 2, r % 4
    cell = a * 256 + i * 64 + (q // 2) * 32 + b * 8 + j * 2 + q % 2
    sel[...] = jnp.where(cell == iota((512, 512), 1), 1.0, 0.0).astype(BF16)

    low128 = iota((128, 128), 1) < 64
    low16 = iota((16, 128), 1) < 64
    low64 = iota((64, 128), 1) < 64

    def to_patches(src, dst, live):
        for h in range(2):
            v = dot(sel[...], src[:, h * 512 : (h + 1) * 512], 1, 1)
            v = jnp.where(live > slot, v, 0.0)
            for half in range(2):
                even, odd = (v[(2 * half + k) * 128 : (2 * half + k + 1) * 128] for k in range(2))
                lanes = slice(half * 128, half * 128 + 128)
                rows = slice(h * 8, h * 8 + 8)
                dst[0, :, rows, lanes] = jnp.where(low128, even, pltpu.roll(odd, 64, 1)).reshape(16, 8, 128)
                dst[1, :, rows, lanes] = jnp.where(low128, pltpu.roll(even, 64, 1), odd).reshape(16, 8, 128)

    slot = iota((1, 128), 1) // 64
    to_patches(act[...], hid, cnt[p])

    def half_of(half):
        return slice(half * 128, half * 128 + 128)

    def slab_of(ref, t):
        return lambda i, j, half: ref[t, 4 * i + j, :, half_of(half)]

    for t in range(2):
        for (kind, half), value in strip_halves(slab_of(hid, t), True).items():
            pool0[2 * p + t, kind, :, half_of(half)] = value.astype(BF16)

    pl.semaphore_wait(barrier, 7)
    for part in range(2):
        launch(0, RIGHT, part)
        launch(0, LEFT, 1 - part)
    share(0, 0)
    share(0, 1)

    spread = jnp.concatenate(
        [jnp.broadcast_to(vm[t].astype(F32), (64, 1024)) for t in range(2)], axis=0
    ).astype(BF16)
    to_patches(spread, msk, 2)
    lane64 = iota((16, 128), 1) % 64
    mask_out = jnp.zeros((16, 128), F32)
    for t in range(2):
        strips = strip_halves(slab_of(msk, t), True)
        for (kind, half), value in strips.items():
            rim_mask[t, kind, :, half_of(half)] = value
            if kind in (TOP, BOTTOM, FIRST, LAST):
                order = (TOP, BOTTOM, FIRST, LAST).index(kind)
                mask_out = jnp.where(lane64 == half * 8 + t * 4 + order, value, mask_out)
    mpool[p] = mask_out.astype(BF16)
    launch(0, RIGHT, MASK)
    launch(0, LEFT, MASK)
    share(0, MASK)

    def twice(w):
        unit = jnp.where(iota((64, 128), 0) == iota((64, 128), 1) % 64, 1.0, 0.0).astype(BF16)
        return dot(w, unit, 0, 0)

    def plane_weights(blk, layer):
        w = twice(pw[blk, layer])
        mirror_in, mirror_out = layer != 1, layer == 1
        for s in range(4):
            for q in range(4):
                u = 2 * (s // 2) + (1 - q // 2 if mirror_in else q // 2)
                v = 2 * (s % 2) + (1 - q % 2 if mirror_in else q % 2)
                rows = slice((s * 4 + q) * 64, (s * 4 + q + 1) * 64)
                for half in range(2):
                    parts = []
                    for col in range(2):
                        dr = u - (1 - half if mirror_out else half)
                        dc = v - (1 - col if mirror_out else col)
                        ok = 0 <= dr < 3 and 0 <= dc < 3
                        tap = dr * 3 + dc
                        parts.append(w[tap * 64 : (tap + 1) * 64] if ok else jnp.zeros((64, 128), F32))
                    weights[blk * 3 + layer, rows, half_of(half)] = jnp.where(low64, *parts).astype(BF16)

    def depth_weights(blk):
        w = twice(dw[blk])
        zero = jnp.zeros((64, 128), F32)
        for tap in range(3):
            part = w[tap * 64 : (tap + 1) * 64]
            if tap == 0:
                part = jnp.where(d > 0, part, 0.0)
            if tap == 2:
                part = jnp.where(d < n_depth - 1, part, 0.0)
            for q in range(4):
                rows = slice(tap * 256 + q * 64, tap * 256 + (q + 1) * 64)
                mine = jnp.where(low64, part, 0.0) if q % 2 == 0 else jnp.where(low64, 0.0, part)
                for half in range(2):
                    dweights[blk, rows, half_of(half)] = (mine if q // 2 == half else zero).astype(BF16)

    def four(v):
        two = jnp.concatenate([v, v], axis=1)
        return jnp.concatenate([two, two], axis=1)

    for blk in range(2):
        for layer in range(3):
            plane_weights(blk, layer)
        depth_weights(blk)
    pass_on(0, 1)
    pass_on(0, 2)
    pass_on(0, 3, 4)
    collect(0)

    group = {NW: BOTTOM, N: BOTTOM, NE: BOTTOM, W: LAST, E: FIRST, SW: TOP, S: TOP, SE: TOP}

    def around_mask(t, carry):
        spot = iota((16, 128), 1) % 64
        found = {}
        for kind in (TOP, BOTTOM, FIRST, LAST):
            order = (TOP, BOTTOM, FIRST, LAST).index(kind)
            ways = [k for k in range(8) if group[k] == kind]
            rows = []
            for k in ways:
                other = nbr[t, k]
                at = jnp.maximum(other, 0)
                keep = (spot % 8) // 4 == jnp.where(other >= 0, at % 2, 2)
                rows.append(jnp.where(keep, mpool[at // 2].astype(F32), 0.0))
            m, n = iota((128, 256), 0), iota((128, 256), 1)
            hit = (m // 64 == (n % 128) // 64) & ((m % 64) // 8 == n // 128) & (m % 4 == order)
            wide = dot(jnp.concatenate(rows, axis=0).astype(BF16), jnp.where(hit, 1.0, 0.0).astype(BF16))
            for at, k in enumerate(ways):
                found[k] = wide[at * 16 : at * 16 + 16]

        def store_odd(i, j, half, value):
            m2[t, i, j, :, half_of(half)] = value

        odd = emit_odd(store_odd, 1, 5)

        def emit(row, half, slabs):
            for j in range(6):
                m1[t, row + 1, j, :, half_of(half)] = slabs[j]
            odd(row, half, slabs)

        surround(slab_of(msk, t), lambda k, kind, half: found[k][:, half_of(half)], 1, emit)
        return carry

    lax.fori_loop(0, 2, around_mask, 0)

    def conv(blk, layer, src, side, mask, dst):
        n = side - 1
        w = weights.at[blk * 3 + layer]
        for lo, hi in ((0, (n + 1) // 2), ((n + 1) // 2, n)):
            rows = (hi - lo) * n * 16
            total = four(pb[layer, blk : blk + 1, :])
            for s in range(4):
                si, sj = s // 2, s % 2
                tap = src[lo + si : hi + si, sj : sj + n].reshape(rows, 256)
                total = total + dot(tap, w[256 * s : 256 * s + 256])
            gated = total * (0.5 + 0.5 * jnp.tanh(0.5 * total)) * mask(lo, hi).reshape(rows, 256)
            dst[lo:hi] = gated.astype(BF16).reshape(hi - lo, n, 16, 256)

    def plane_layers(blk, tile, halo):
        def store_odd(i, j, half, value):
            x_in[i, j, :, half_of(half)] = value.astype(BF16)

        def strip(k, kind, half):
            if not halo:
                return jnp.zeros((16, 128), F32)
            other = nbr[tile, k]
            value = pools[blk][jnp.maximum(other, 0), kind, :, half_of(half)].astype(F32)
            return jnp.where(other >= 0, value, 0.0)

        surround(slab_of(hid, tile), strip, 2, emit_odd(store_odd, 2, 7))
        conv(blk, 0, x_in, 7, lambda lo, hi: m1[tile, lo:hi], y1)
        conv(blk, 1, y1, 6, lambda lo, hi: m2[tile, lo:hi], y2)
        conv(blk, 2, y2, 5, lambda lo, hi: msk[tile, 4 * lo : 4 * hi], y3)

    def send_rim(blk, tile):
        slab = lambda i, j, half: y3[i, j, :, half_of(half)].astype(F32)
        for (kind, half), value in strip_halves(slab, True).items():
            rim[blk, tile, kind, :, half_of(half)] = value.astype(BF16)
        for way in range(2):
            rim_copy(blk, way, tile).start()

    def first_block(tile, carry):
        plane_layers(0, tile, True)
        branch[0, tile] = y3[...]
        send_rim(0, tile)
        return carry

    def early_block(tile, carry):
        plane_layers(1, tile, False)
        branch[1, tile] = y3[...]
        for way in range(2):
            full_copy(1, way, tile).start()
        return carry

    def second_block(tile, carry):
        plane_layers(1, tile, True)
        send_rim(1, tile)
        return carry

    def along_depth(blk, below, own, above):
        return dot(jnp.concatenate([below, own, above], axis=1), dweights[blk]) + four(db[blk : blk + 1, :])

    def residual(blk, t):
        for way in range(2):
            full_copy(blk, way, t).wait_recv()
        total = along_depth(
            blk, full_in[blk, 0, t].reshape(256, 256), branch[blk, t].reshape(256, 256),
            full_in[blk, 1, t].reshape(256, 256),
        )
        new = hid[t].reshape(256, 256) + msk[t].reshape(256, 256) * total
        hid[t] = new.astype(BF16).astype(F32).reshape(16, 16, 256)

    def rim_residual(blk, t):
        for way in range(2):
            rim_copy(blk, way, t).wait_recv()
        total = along_depth(
            blk, rim_in[blk, 0, t].reshape(96, 256), rim[blk, t].reshape(96, 256), rim_in[blk, 1, t].reshape(96, 256)
        )
        old = pools[blk][2 * p + t].astype(F32).reshape(96, 256)
        return (old + rim_mask[t].reshape(96, 256) * total).astype(BF16).reshape(6, 16, 256)

    def put_rim(t, strips):
        row = iota((16, 1), 0)
        first, last, top, bottom = row % 4 == 0, row % 4 == 3, row < 4, row >= 12
        high16 = iota((16, 128), 1) >= 64
        for half in range(2):
            kinds = [strips[kind, :, half_of(half)].astype(F32) for kind in range(6)]
            for i in range(4):
                for j in range(4):
                    value = new = hid[t, 4 * i + j, :, half_of(half)]
                    if j == 0:
                        new = jnp.where(first, turn(kinds[FIRST], -i), new)
                    if j == 3:
                        new = jnp.where(last, turn(kinds[LAST], 3 - i), new)
                    if j == 1:
                        new = jnp.where(first, jnp.where(high16, value, turn(kinds[COLS2], -i)), new)
                    if j == 2:
                        new = jnp.where(last, jnp.where(high16, turn(kinds[COLS2], 3 - i), value), new)
                    if i == 0 or (i == 1 and half == 0):
                        new = jnp.where(top, turn(kinds[TOP if i == 0 else ROWS2], -4 * j), new)
                    if i == 3 or (i == 2 and half == 1):
                        new = jnp.where(bottom, turn(kinds[BOTTOM if i == 3 else ROWS2], 12 - 4 * j), new)
                    if new is not value:
                        hid[t, 4 * i + j, :, half_of(half)] = new

    lax.fori_loop(0, 2, first_block, 0)
    for t in range(2):
        for way in range(2):
            full_copy(0, way, t).start()
    for t in range(2):
        pool1[2 * p + t] = rim_residual(0, t)
        launch(1, RIGHT if t == 0 else LEFT, t)
    launch(1, RIGHT, 1)
    launch(1, LEFT, 0)
    share(1, 0)
    share(1, 1)
    pass_on(1, 1)
    pass_on(1, 2)
    for t in range(2):
        residual(0, t)
    lax.fori_loop(0, 2, early_block, 0)
    pass_on(1, 3, 4)
    collect(1)
    lax.fori_loop(0, 2, second_block, 0)
    for t in range(2):
        residual(1, t)
    for t in range(2):
        put_rim(t, rim_residual(1, t))

    for h in range(2):
        parts = []
        for half in range(2):
            lanes, rows = half_of(half), slice(h * 8, h * 8 + 8)
            one = hid[0, :, rows, lanes].reshape(128, 128)
            two = hid[1, :, rows, lanes].reshape(128, 128)
            parts.append(jnp.where(low128, one, pltpu.roll(two, 64, 1)))
            parts.append(jnp.where(low128, pltpu.roll(one, 64, 1), two))
        back = dot(jnp.concatenate(parts, axis=0).astype(BF16), sel[...], 0, 0)
        out[:, h * 512 : (h + 1) * 512] = back.astype(BF16)

    settle(0)
    settle(1)
    for t in range(2):
        for way in range(2):
            for blk in range(2):
                rim_copy(blk, way, t).wait_send()
                full_copy(blk, way, t).wait_send()


def shards(mesh, activations, plane_weight, plane_bias, depth_weight, depth_bias, counts, neighbours, voxel_mask):
    n_depth, n_plane = mesh.shape["depth"], mesh.shape["plane"]
    vmem = pl.BlockSpec(memory_space=pltpu.VMEM)
    smem = pl.BlockSpec(memory_space=pltpu.SMEM)
    dma = pltpu.SemaphoreType.DMA
    out = pl.pallas_call(
        functools.partial(body, n_depth, n_plane),
        out_shape=jax.ShapeDtypeStruct((128, 1024), BF16),
        in_specs=[vmem] * 5 + [smem, smem, vmem],
        out_specs=vmem,
        scratch_shapes=[
            pltpu.VMEM((512, 512), BF16),
            pltpu.VMEM((2, 16, 16, 256), F32),
            pltpu.VMEM((2, 16, 16, 256), F32),
            pltpu.VMEM((7, 7, 16, 256), BF16),
            pltpu.VMEM((6, 6, 16, 256), BF16),
            pltpu.VMEM((5, 5, 16, 256), BF16),
            pltpu.VMEM((4, 4, 16, 256), BF16),
            pltpu.VMEM((2, 2, 4, 4, 16, 256), BF16),
            pltpu.VMEM((2, 6, 6, 16, 256), F32),
            pltpu.VMEM((2, 5, 5, 16, 256), F32),
            pltpu.VMEM((6, 1024, 256), BF16),
            pltpu.VMEM((2, 768, 256), BF16),
            pltpu.VMEM((2 * n_plane, 6, 16, 256), BF16),
            pltpu.VMEM((2 * n_plane, 6, 16, 256), BF16),
            pltpu.VMEM((n_plane, 16, 128), BF16),
            pltpu.VMEM((2, 2, 6, 16, 256), BF16),
            pltpu.VMEM((2, 2, 2, 6, 16, 256), BF16),
            pltpu.VMEM((2, 6, 16, 256), F32),
            pltpu.VMEM((2, 2, 2, 4, 4, 16, 256), BF16),
            dma((2, 2, 4, 3)),
            dma((2, 2, 4, 3)),
            dma((2, 9, 3)),
            dma((2, 9, 3)),
            dma((2, 2, 2)),
            dma((2, 2, 2)),
            dma((2, 2, 2)),
            dma((2, 2, 2)),
        ],
        compiler_params=pltpu.CompilerParams(
            collective_id=0, has_side_effects=True, vmem_limit_bytes=56 * 2**20
        ),
    )(
        activations.reshape(128, 1024), plane_weight, plane_bias.transpose(1, 0, 2), depth_weight, depth_bias, counts, neighbours,
        voxel_mask,
    )
    return out.reshape(activations.shape)


def solution(mesh):
    in_specs = (
        P("plane", "depth", None, None),
        P(),
        P(),
        P(),
        P(),
        P(),
        P("plane", None),
        P("plane", "depth", None),
    )
    out_specs = P("plane", "depth", None, None)
    return jax.shard_map(
        functools.partial(shards, mesh), mesh=mesh, in_specs=in_specs, out_specs=out_specs, check_vma=False
    )
```

```python
import functools

import jax
import jax.numpy as jnp
from jax import lax
from jax.experimental import pallas as pl
from jax.experimental.pallas import tpu as pltpu
from jax.sharding import PartitionSpec as P


F32, BF16 = jnp.float32, jnp.bfloat16
MESH = pl.DeviceIdType.MESH
RIGHT, LEFT = 0, 1
MASK = 12
NW, N, NE, W, E, SW, S, SE = range(8)
TOP, BOTTOM, ROWS2, FIRST, LAST, COLS2 = range(6)


def iota(shape, dim):
    return lax.broadcasted_iota(jnp.int32, shape, dim)


def turn(x, k):
    k %= 16
    return pltpu.roll(x, k, 0) if k else x


def dot(a, b, ca=1, cb=0):
    return lax.dot_general(a, b, (((ca,), (cb,)), ((), ())), preferred_element_type=F32)


def row_strip(slab, a):
    row = iota((16, 1), 0)
    out = turn(slab(0), -4 * a)
    for j in range(1, 4):
        out = jnp.where(row // 4 == j, turn(slab(j), 4 * j - 4 * a), out)
    return out


def col_strip(slab, b):
    row = iota((16, 1), 0)
    out = turn(slab(0), -b)
    for i in range(1, 4):
        out = jnp.where(row % 4 == i, turn(slab(i), i - b), out)
    return out


def strip_halves(slab, wide):
    low = iota((16, 128), 1) < 64
    out = {}
    for half in range(2):
        out[TOP, half] = row_strip(lambda j: slab(0, j, half), 0)
        out[BOTTOM, half] = row_strip(lambda j: slab(3, j, half), 3)
        out[FIRST, half] = col_strip(lambda i: slab(i, 0, half), 0)
        out[LAST, half] = col_strip(lambda i: slab(i, 3, half), 3)
        if wide:
            if half == 0:
                out[ROWS2, half] = row_strip(lambda j: slab(1, j, half), 0)
            else:
                out[ROWS2, half] = row_strip(lambda j: slab(2, j, half), 3)
            out[COLS2, half] = jnp.where(
                low, col_strip(lambda i: slab(i, 1, half), 0), col_strip(lambda i: slab(i, 2, half), 3)
            )
    return out


def surround(slab, strip, width, emit):
    row = iota((16, 1), 0)
    first, last = row % 4 == 0, row % 4 == 3
    top, bottom = row < 4, row >= 12
    cols = range(-width, 4 + width)
    for half in range(2):

        def widened(i):
            out = {j: slab(i, j, half) for j in range(4)}
            for j in cols:
                if j == -1:
                    out[j] = jnp.where(first, turn(strip(W, LAST, half), -i), turn(slab(i, 3, half), 1))
                if j == -2:
                    out[j] = jnp.where(first, turn(strip(W, COLS2, half), -i), turn(slab(i, 2, half), 1))
                if j == 4:
                    out[j] = jnp.where(last, turn(strip(E, FIRST, half), 3 - i), turn(slab(i, 0, half), -1))
                if j == 5:
                    out[j] = jnp.where(last, turn(strip(E, COLS2, half), 3 - i), turn(slab(i, 1, half), -1))
            return out

        def beyond(kind, mid, before, after, base, j):
            own = strip(mid, kind, half)
            if 0 <= j < 4:
                return turn(own, base - 4 * j)
            if j == -1:
                return jnp.where(first, turn(strip(before, kind, half), base + 1), turn(own, base - 11))
            if j == -2:
                return jnp.where(first, turn(strip(before, kind, half), base - 11), turn(own, base - 7))
            if j == 4:
                return jnp.where(last, turn(strip(after, kind, half), base + 3), turn(own, base - 1))
            return jnp.where(last, turn(strip(after, kind, half), base - 1), turn(own, base - 5))

        for i in range(4):
            line = widened(i)
            emit(i, half, [line[j] for j in cols])
            if i == 0:
                emit(4, half, [
                    jnp.where(bottom, beyond(TOP, S, SW, SE, 12, j), turn(line[j], -4)) for j in cols
                ])
            if i == 1 and width == 2 and half == 0:
                emit(5, half, [
                    jnp.where(bottom, beyond(ROWS2, S, SW, SE, 12, j), turn(line[j], -4)) for j in cols
                ])
            if i == 2 and width == 2 and half == 1:
                emit(-2, half, [
                    jnp.where(top, beyond(ROWS2, N, NW, NE, 0, j), turn(line[j], 4)) for j in cols
                ])
            if i == 3:
                emit(-1, half, [
                    jnp.where(top, beyond(BOTTOM, N, NW, NE, 0, j), turn(line[j], 4)) for j in cols
                ])


def emit_odd(store, width, side):
    def emit(row, half, slabs):
        low = iota((16, 128), 1) < 64
        i = row + width - (1 - half)
        if 0 <= i < side:
            for j in range(side):
                store(i, j, half, jnp.where(low, slabs[j + 1], slabs[j]))

    return emit


def body(
    n_depth, n_plane,
    act_any, pw_any, pb, dw_any, db, cnt, nbr, vm_any, out,
    act, pw, dw, vm, load_sem,
    sel, hid, msk, x_in, y1, y2, y3, branch, m1, m2, weights, dweights,
    pool0, pool1, rim, rim_in, rim_mask, full_in,
    ring_ss, ring_rs, sib_ss, sib_rs, rim_ss, rim_rs, full_ss, full_rs,
):
    n_z = n_plane // 2
    pools = (pool0, pool1)
    d = lax.axis_index("depth")
    p = lax.axis_index("plane")
    z, c = p // 2, p % 2

    def z_at(offset):
        return lax.rem(z + offset + n_z, n_z)

    def plane_id(offset, core):
        return z_at(offset) * 2 + core

    def depth_id(way):
        return lax.rem(d + (1 if way == 0 else n_depth - 1), n_depth)

    loads = [
        pltpu.make_async_copy(src, dst, load_sem.at[k])
        for k, (src, dst) in enumerate(((act_any, act), (vm_any, vm), (pw_any, pw), (dw_any, dw)))
    ]
    for load in loads:
        load.start()
    barrier = pltpu.get_barrier_semaphore()
    for target in (
        {"plane": plane_id(1, 1 - c)}, {"plane": plane_id(-1, 1 - c)}, {"plane": z * 2 + 1 - c},
        {"plane": plane_id(2, c)}, {"plane": plane_id(-2, c)},
        {"depth": depth_id(0)}, {"depth": depth_id(1)},
    ):
        pl.semaphore_signal(barrier, inc=1, device_id=target, device_id_type=MESH)

    def block_ref(g, owner, item):
        return pools[g].at[owner, pl.ds(6 * item, 7 if g == 0 and item == 1 else 6)]

    def core_at(dist):
        return 1 - c if dist % 2 else c

    def ring_copy(g, way, k, m, item, owner_at):
        sign = -1 if way == RIGHT else 1
        ref = block_ref(g, plane_id(sign * owner_at, core_at(owner_at)), item)
        return pltpu.make_async_remote_copy(
            src_ref=ref, dst_ref=ref, send_sem=ring_ss.at[g, way, k + m - 1, item],
            recv_sem=ring_rs.at[g, way, k + m - 1, item],
            device_id={"plane": plane_id(-sign * m, core_at(m))}, device_id_type=MESH,
        )

    def ring_out(g, way, k, m, item):
        return ring_copy(g, way, k, m, item, k)

    def ring_in(g, way, dist, item):
        return ring_copy(g, way, dist - 1, 1, item, dist)

    def sib_copy(g, way, dist, item, mine):
        core = core_at(dist) if mine else 1 - core_at(dist)
        owner = plane_id(-dist if way == RIGHT else dist, core)
        key = 0 if dist == 0 else way * 4 + dist
        ref = block_ref(g, owner, item)
        return pltpu.make_async_remote_copy(
            src_ref=ref, dst_ref=ref, send_sem=sib_ss.at[g, key, item], recv_sem=sib_rs.at[g, key, item],
            device_id={"plane": z * 2 + 1 - c}, device_id_type=MESH,
        )

    def leads(way):
        return 0 if way == RIGHT else 1

    def items(g, way, dist):
        got = (leads(way), 1 - leads(way))
        if dist == 4:
            got = got[:1]
        return got

    def onward(g, way, dist, item):
        got = []
        if dist == 2 and item in items(g, way, 4):
            got.append(ring_out(g, way, 2, 2, item))
        if dist < 3:
            got.append(ring_out(g, way, dist, 1, item))
        return got

    def launch(g, way, item):
        for copy in onward(g, way, 0, item):
            copy.start()

    def share(g, item):
        sib_copy(g, RIGHT, 0, item, True).start()

    def pass_on(g, *dists):
        order = sorted(
            (items(g, way, dist).index(item), dist, way, item)
            for dist in dists for way in (RIGHT, LEFT) for item in items(g, way, dist)
        )
        for _, dist, way, item in order:
            ring_in(g, way, dist, item).wait_recv()
            for copy in onward(g, way, dist, item):
                copy.start()
            sib_copy(g, way, dist, item, True).start()

    def everything(g):
        got = [(RIGHT, 0, item) for item in (0, 1)]
        return got + [(way, dist, item) for dist in range(1, 5) for way in (RIGHT, LEFT) for item in items(g, way, dist)]

    def collect(g):
        for way, dist, item in everything(g):
            sib_copy(g, way, dist, item, False).wait_recv()

    def settle(g):
        for way, dist, item in everything(g):
            sib_copy(g, way, dist, item, True).wait_send()
        for dist in range(3):
            for way in (RIGHT, LEFT):
                for item in items(g, way, max(dist, 1)):
                    for copy in onward(g, way, dist, item):
                        copy.wait_send()

    def rim_copy(blk, way, t):
        return pltpu.make_async_remote_copy(
            src_ref=rim.at[blk, t], dst_ref=rim_in.at[blk, way, t],
            send_sem=rim_ss.at[blk, way, t], recv_sem=rim_rs.at[blk, way, t],
            device_id={"depth": depth_id(way)}, device_id_type=MESH,
        )

    def full_copy(blk, way, t):
        return pltpu.make_async_remote_copy(
            src_ref=branch.at[blk, t], dst_ref=full_in.at[blk, way, t],
            send_sem=full_ss.at[blk, way, t], recv_sem=full_rs.at[blk, way, t],
            device_id={"depth": depth_id(way)}, device_id_type=MESH,
        )

    r = iota((512, 1), 0)
    q, i, j, a, b = r // 128, (r // 32) % 4, (r // 8) % 4, (r // 4) % 2, r % 4
    cell = a * 256 + i * 64 + (q // 2) * 32 + b * 8 + j * 2 + q % 2
    sel[...] = jnp.where(cell == iota((512, 512), 1), 1.0, 0.0).astype(BF16)

    low128 = iota((128, 128), 1) < 64
    low16 = iota((16, 128), 1) < 64
    low64 = iota((64, 128), 1) < 64

    def to_patches(src, dst, live):
        for h in range(2):
            v = dot(sel[...], src[:, h * 512 : (h + 1) * 512], 1, 1)
            v = jnp.where(live > slot, v, 0.0)
            for half in range(2):
                even, odd = (v[(2 * half + k) * 128 : (2 * half + k + 1) * 128] for k in range(2))
                lanes = slice(half * 128, half * 128 + 128)
                rows = slice(h * 8, h * 8 + 8)
                dst[0, :, rows, lanes] = jnp.where(low128, even, pltpu.roll(odd, 64, 1)).reshape(16, 8, 128)
                dst[1, :, rows, lanes] = jnp.where(low128, pltpu.roll(even, 64, 1), odd).reshape(16, 8, 128)

    slot = iota((1, 128), 1) // 64
    loads[0].wait()
    to_patches(act[...], hid, cnt[p])

    def half_of(half):
        return slice(half * 128, half * 128 + 128)

    def slab_of(ref, t):
        return lambda i, j, half: ref[t, 4 * i + j, :, half_of(half)]

    for t in range(2):
        for (kind, half), value in strip_halves(slab_of(hid, t), True).items():
            pool0[p, 6 * t + kind, :, half_of(half)] = value.astype(BF16)

    loads[1].wait()
    spread = jnp.concatenate(
        [jnp.broadcast_to(vm[t].astype(F32), (64, 1024)) for t in range(2)], axis=0
    ).astype(BF16)
    to_patches(spread, msk, 2)
    lane64 = iota((16, 128), 1) % 64
    mask_out = jnp.zeros((16, 128), F32)
    for t in range(2):
        strips = strip_halves(slab_of(msk, t), True)
        for (kind, half), value in strips.items():
            rim_mask[t, kind, :, half_of(half)] = value
            if kind in (TOP, BOTTOM, FIRST, LAST):
                order = (TOP, BOTTOM, FIRST, LAST).index(kind)
                mask_out = jnp.where(lane64 == half * 8 + t * 4 + order, value, mask_out)
    pool0[p, MASK] = jnp.concatenate([mask_out, jnp.zeros((16, 128), F32)], axis=1).astype(BF16)

    pl.semaphore_wait(barrier, 7)
    for item in range(2):
        launch(0, RIGHT, item)
        launch(0, LEFT, 1 - item)
    share(0, 0)
    share(0, 1)

    def twice(w):
        unit = jnp.where(iota((64, 128), 0) == iota((64, 128), 1) % 64, 1.0, 0.0).astype(BF16)
        return dot(w, unit, 0, 0)

    def plane_weights(blk, layer):
        w = twice(pw[blk, layer])
        mirror_in, mirror_out = layer != 1, layer == 1
        for s in range(4):
            for q in range(4):
                u = 2 * (s // 2) + (1 - q // 2 if mirror_in else q // 2)
                v = 2 * (s % 2) + (1 - q % 2 if mirror_in else q % 2)
                rows = slice((s * 4 + q) * 64, (s * 4 + q + 1) * 64)
                for half in range(2):
                    parts = []
                    for col in range(2):
                        dr = u - (1 - half if mirror_out else half)
                        dc = v - (1 - col if mirror_out else col)
                        ok = 0 <= dr < 3 and 0 <= dc < 3
                        tap = dr * 3 + dc
                        parts.append(w[tap * 64 : (tap + 1) * 64] if ok else jnp.zeros((64, 128), F32))
                    weights[blk * 3 + layer, rows, half_of(half)] = jnp.where(low64, *parts).astype(BF16)

    def depth_weights(blk):
        w = twice(dw[blk])
        zero = jnp.zeros((64, 128), F32)
        for tap in range(3):
            part = w[tap * 64 : (tap + 1) * 64]
            if tap == 0:
                part = jnp.where(d > 0, part, 0.0)
            if tap == 2:
                part = jnp.where(d < n_depth - 1, part, 0.0)
            for q in range(4):
                rows = slice(tap * 256 + q * 64, tap * 256 + (q + 1) * 64)
                mine = jnp.where(low64, part, 0.0) if q % 2 == 0 else jnp.where(low64, 0.0, part)
                for half in range(2):
                    dweights[blk, rows, half_of(half)] = (mine if q // 2 == half else zero).astype(BF16)

    def four(v):
        two = jnp.concatenate([v, v], axis=1)
        return jnp.concatenate([two, two], axis=1)

    loads[2].wait()
    loads[3].wait()
    for blk in range(2):
        for layer in range(3):
            plane_weights(blk, layer)
        depth_weights(blk)
    pass_on(0, 1)
    pass_on(0, 2)
    pass_on(0, 3, 4)
    collect(0)

    group = {NW: BOTTOM, N: BOTTOM, NE: BOTTOM, W: LAST, E: FIRST, SW: TOP, S: TOP, SE: TOP}

    def around_mask(t, carry):
        spot = iota((16, 128), 1) % 64
        found = {}
        for kind in (TOP, BOTTOM, FIRST, LAST):
            order = (TOP, BOTTOM, FIRST, LAST).index(kind)
            ways = [k for k in range(8) if group[k] == kind]
            rows = []
            for k in ways:
                other = nbr[t, k]
                at = jnp.maximum(other, 0)
                keep = (spot % 8) // 4 == jnp.where(other >= 0, at % 2, 2)
                rows.append(jnp.where(keep, pool0[at // 2, MASK, :, :128].astype(F32), 0.0))
            m, n = iota((128, 256), 0), iota((128, 256), 1)
            hit = (m // 64 == (n % 128) // 64) & ((m % 64) // 8 == n // 128) & (m % 4 == order)
            wide = dot(jnp.concatenate(rows, axis=0).astype(BF16), jnp.where(hit, 1.0, 0.0).astype(BF16))
            for at, k in enumerate(ways):
                found[k] = wide[at * 16 : at * 16 + 16]

        def store_odd(i, j, half, value):
            m2[t, i, j, :, half_of(half)] = value

        odd = emit_odd(store_odd, 1, 5)

        def emit(row, half, slabs):
            for j in range(6):
                m1[t, row + 1, j, :, half_of(half)] = slabs[j]
            odd(row, half, slabs)

        surround(slab_of(msk, t), lambda k, kind, half: found[k][:, half_of(half)], 1, emit)
        return carry

    lax.fori_loop(0, 2, around_mask, 0)

    def conv(blk, layer, src, side, mask, dst):
        n = side - 1
        w = weights.at[blk * 3 + layer]
        for lo, hi in ((0, (n + 1) // 2), ((n + 1) // 2, n)):
            rows = (hi - lo) * n * 16
            total = four(pb[layer, blk : blk + 1, :])
            for s in range(4):
                si, sj = s // 2, s % 2
                tap = src[lo + si : hi + si, sj : sj + n].reshape(rows, 256)
                total = total + dot(tap, w[256 * s : 256 * s + 256])
            gated = total * (0.5 + 0.5 * jnp.tanh(0.5 * total)) * mask(lo, hi).reshape(rows, 256)
            dst[lo:hi] = gated.astype(BF16).reshape(hi - lo, n, 16, 256)

    def plane_layers(blk, tile, halo):
        def store_odd(i, j, half, value):
            x_in[i, j, :, half_of(half)] = value.astype(BF16)

        def strip(k, kind, half):
            if not halo:
                return jnp.zeros((16, 128), F32)
            other = nbr[tile, k]
            at = jnp.maximum(other, 0)
            value = pools[blk][at // 2, at % 2 * 6 + kind, :, half_of(half)].astype(F32)
            return jnp.where(other >= 0, value, 0.0)

        surround(slab_of(hid, tile), strip, 2, emit_odd(store_odd, 2, 7))
        conv(blk, 0, x_in, 7, lambda lo, hi: m1[tile, lo:hi], y1)
        conv(blk, 1, y1, 6, lambda lo, hi: m2[tile, lo:hi], y2)
        conv(blk, 2, y2, 5, lambda lo, hi: msk[tile, 4 * lo : 4 * hi], y3)

    def send_rim(blk, tile):
        slab = lambda i, j, half: y3[i, j, :, half_of(half)].astype(F32)
        for (kind, half), value in strip_halves(slab, True).items():
            rim[blk, tile, kind, :, half_of(half)] = value.astype(BF16)
        for way in range(2):
            rim_copy(blk, way, tile).start()

    def first_block(tile, carry):
        plane_layers(0, tile, True)
        branch[0, tile] = y3[...]
        send_rim(0, tile)
        return carry

    def early_block(tile, carry):
        plane_layers(1, tile, False)
        branch[1, tile] = y3[...]
        for way in range(2):
            full_copy(1, way, tile).start()
        return carry

    def second_block(tile, carry):
        plane_layers(1, tile, True)
        send_rim(1, tile)
        return carry

    def along_depth(blk, below, own, above):
        return dot(jnp.concatenate([below, own, above], axis=1), dweights[blk]) + four(db[blk : blk + 1, :])

    def residual(blk, t):
        for way in range(2):
            full_copy(blk, way, t).wait_recv()
        total = along_depth(
            blk, full_in[blk, 0, t].reshape(256, 256), branch[blk, t].reshape(256, 256),
            full_in[blk, 1, t].reshape(256, 256),
        )
        new = hid[t].reshape(256, 256) + msk[t].reshape(256, 256) * total
        hid[t] = new.astype(BF16).astype(F32).reshape(16, 16, 256)

    def rim_residual(blk, t):
        for way in range(2):
            rim_copy(blk, way, t).wait_recv()
        total = along_depth(
            blk, rim_in[blk, 0, t].reshape(96, 256), rim[blk, t].reshape(96, 256), rim_in[blk, 1, t].reshape(96, 256)
        )
        old = pools[blk][p, 6 * t : 6 * t + 6].astype(F32).reshape(96, 256)
        return (old + rim_mask[t].reshape(96, 256) * total).astype(BF16).reshape(6, 16, 256)

    def put_rim(t, strips):
        row = iota((16, 1), 0)
        first, last, top, bottom = row % 4 == 0, row % 4 == 3, row < 4, row >= 12
        high16 = iota((16, 128), 1) >= 64
        for half in range(2):
            kinds = [strips[kind, :, half_of(half)].astype(F32) for kind in range(6)]
            for i in range(4):
                for j in range(4):
                    value = new = hid[t, 4 * i + j, :, half_of(half)]
                    if j == 0:
                        new = jnp.where(first, turn(kinds[FIRST], -i), new)
                    if j == 3:
                        new = jnp.where(last, turn(kinds[LAST], 3 - i), new)
                    if j == 1:
                        new = jnp.where(first, jnp.where(high16, value, turn(kinds[COLS2], -i)), new)
                    if j == 2:
                        new = jnp.where(last, jnp.where(high16, turn(kinds[COLS2], 3 - i), value), new)
                    if i == 0 or (i == 1 and half == 0):
                        new = jnp.where(top, turn(kinds[TOP if i == 0 else ROWS2], -4 * j), new)
                    if i == 3 or (i == 2 and half == 1):
                        new = jnp.where(bottom, turn(kinds[BOTTOM if i == 3 else ROWS2], 12 - 4 * j), new)
                    if new is not value:
                        hid[t, 4 * i + j, :, half_of(half)] = new

    lax.fori_loop(0, 2, first_block, 0)
    for t in range(2):
        for way in range(2):
            full_copy(0, way, t).start()
    for t in range(2):
        pool1[p, 6 * t : 6 * t + 6] = rim_residual(0, t)
        launch(1, RIGHT if t == 0 else LEFT, t)
    launch(1, RIGHT, 1)
    launch(1, LEFT, 0)
    share(1, 0)
    share(1, 1)
    pass_on(1, 1)
    pass_on(1, 2)
    for t in range(2):
        residual(0, t)
    lax.fori_loop(0, 2, early_block, 0)
    pass_on(1, 3, 4)
    collect(1)
    lax.fori_loop(0, 2, second_block, 0)
    for t in range(2):
        residual(1, t)
    for t in range(2):
        put_rim(t, rim_residual(1, t))

    for h in range(2):
        parts = []
        for half in range(2):
            lanes, rows = half_of(half), slice(h * 8, h * 8 + 8)
            one = hid[0, :, rows, lanes].reshape(128, 128)
            two = hid[1, :, rows, lanes].reshape(128, 128)
            parts.append(jnp.where(low128, one, pltpu.roll(two, 64, 1)))
            parts.append(jnp.where(low128, pltpu.roll(one, 64, 1), two))
        back = dot(jnp.concatenate(parts, axis=0).astype(BF16), sel[...], 0, 0)
        out[:, h * 512 : (h + 1) * 512] = back.astype(BF16)

    settle(0)
    settle(1)
    for t in range(2):
        for way in range(2):
            for blk in range(2):
                rim_copy(blk, way, t).wait_send()
                full_copy(blk, way, t).wait_send()


def shards(mesh, activations, plane_weight, plane_bias, depth_weight, depth_bias, counts, neighbours, voxel_mask):
    n_depth, n_plane = mesh.shape["depth"], mesh.shape["plane"]
    vmem = pl.BlockSpec(memory_space=pltpu.VMEM)
    smem = pl.BlockSpec(memory_space=pltpu.SMEM)
    hbm = pl.BlockSpec(memory_space=pl.ANY)
    dma = pltpu.SemaphoreType.DMA
    out = pl.pallas_call(
        functools.partial(body, n_depth, n_plane),
        out_shape=jax.ShapeDtypeStruct((128, 1024), BF16),
        in_specs=[hbm, hbm, vmem, hbm, vmem, smem, smem, hbm],
        out_specs=vmem,
        scratch_shapes=[
            pltpu.VMEM((128, 1024), BF16),
            pltpu.VMEM(plane_weight.shape, BF16),
            pltpu.VMEM(depth_weight.shape, BF16),
            pltpu.VMEM((2, 1, 1024), jnp.int32),
            dma((4,)),
            pltpu.VMEM((512, 512), BF16),
            pltpu.VMEM((2, 16, 16, 256), F32),
            pltpu.VMEM((2, 16, 16, 256), F32),
            pltpu.VMEM((7, 7, 16, 256), BF16),
            pltpu.VMEM((6, 6, 16, 256), BF16),
            pltpu.VMEM((5, 5, 16, 256), BF16),
            pltpu.VMEM((4, 4, 16, 256), BF16),
            pltpu.VMEM((2, 2, 4, 4, 16, 256), BF16),
            pltpu.VMEM((2, 6, 6, 16, 256), F32),
            pltpu.VMEM((2, 5, 5, 16, 256), F32),
            pltpu.VMEM((6, 1024, 256), BF16),
            pltpu.VMEM((2, 768, 256), BF16),
            pltpu.VMEM((n_plane, 13, 16, 256), BF16),
            pltpu.VMEM((n_plane, 12, 16, 256), BF16),
            pltpu.VMEM((2, 2, 6, 16, 256), BF16),
            pltpu.VMEM((2, 2, 2, 6, 16, 256), BF16),
            pltpu.VMEM((2, 6, 16, 256), F32),
            pltpu.VMEM((2, 2, 2, 4, 4, 16, 256), BF16),
            dma((2, 2, 4, 2)),
            dma((2, 2, 4, 2)),
            dma((2, 9, 2)),
            dma((2, 9, 2)),
            dma((2, 2, 2)),
            dma((2, 2, 2)),
            dma((2, 2, 2)),
            dma((2, 2, 2)),
        ],
        compiler_params=pltpu.CompilerParams(
            collective_id=0, has_side_effects=True, vmem_limit_bytes=56 * 2**20
        ),
    )(
        activations.reshape(128, 1024), plane_weight, plane_bias.transpose(1, 0, 2), depth_weight, depth_bias, counts, neighbours,
        voxel_mask,
    )
    return out.reshape(activations.shape)


def solution(mesh):
    in_specs = (
        P("plane", "depth", None, None),
        P(),
        P(),
        P(),
        P(),
        P(),
        P("plane", None),
        P("plane", "depth", None),
    )
    out_specs = P("plane", "depth", None, None)
    return jax.shard_map(
        functools.partial(shards, mesh), mesh=mesh, in_specs=in_specs, out_specs=out_specs, check_vma=False
    )
```

```python
import functools

import jax
import jax.numpy as jnp
from jax import lax
from jax.experimental import pallas as pl
from jax.experimental.pallas import tpu as pltpu
from jax.sharding import PartitionSpec as P


F32, BF16 = jnp.float32, jnp.bfloat16
MESH = pl.DeviceIdType.MESH
RIGHT, LEFT = 0, 1
MASK = 12
NW, N, NE, W, E, SW, S, SE = range(8)
TOP, BOTTOM, ROWS2, FIRST, LAST, COLS2 = range(6)


def iota(shape, dim):
    return lax.broadcasted_iota(jnp.int32, shape, dim)


def turn(x, k):
    k %= 16
    return pltpu.roll(x, k, 0) if k else x


def dot(a, b, ca=1, cb=0):
    return lax.dot_general(a, b, (((ca,), (cb,)), ((), ())), preferred_element_type=F32)


def row_strip(slab, a):
    row = iota((16, 1), 0)
    out = turn(slab(0), -4 * a)
    for j in range(1, 4):
        out = jnp.where(row // 4 == j, turn(slab(j), 4 * j - 4 * a), out)
    return out


def col_strip(slab, b):
    row = iota((16, 1), 0)
    out = turn(slab(0), -b)
    for i in range(1, 4):
        out = jnp.where(row % 4 == i, turn(slab(i), i - b), out)
    return out


def strip_halves(slab, wide):
    low = iota((16, 128), 1) < 64
    out = {}
    for half in range(2):
        out[TOP, half] = row_strip(lambda j: slab(0, j, half), 0)
        out[BOTTOM, half] = row_strip(lambda j: slab(3, j, half), 3)
        out[FIRST, half] = col_strip(lambda i: slab(i, 0, half), 0)
        out[LAST, half] = col_strip(lambda i: slab(i, 3, half), 3)
        if wide:
            if half == 0:
                out[ROWS2, half] = row_strip(lambda j: slab(1, j, half), 0)
            else:
                out[ROWS2, half] = row_strip(lambda j: slab(2, j, half), 3)
            out[COLS2, half] = jnp.where(
                low, col_strip(lambda i: slab(i, 1, half), 0), col_strip(lambda i: slab(i, 2, half), 3)
            )
    return out


def surround(slab, strip, width, emit):
    row = iota((16, 1), 0)
    first, last = row % 4 == 0, row % 4 == 3
    top, bottom = row < 4, row >= 12
    cols = range(-width, 4 + width)
    for half in range(2):

        def widened(i):
            out = {j: slab(i, j, half) for j in range(4)}
            for j in cols:
                if j == -1:
                    out[j] = jnp.where(first, turn(strip(W, LAST, half), -i), turn(slab(i, 3, half), 1))
                if j == -2:
                    out[j] = jnp.where(first, turn(strip(W, COLS2, half), -i), turn(slab(i, 2, half), 1))
                if j == 4:
                    out[j] = jnp.where(last, turn(strip(E, FIRST, half), 3 - i), turn(slab(i, 0, half), -1))
                if j == 5:
                    out[j] = jnp.where(last, turn(strip(E, COLS2, half), 3 - i), turn(slab(i, 1, half), -1))
            return out

        def beyond(kind, mid, before, after, base, j):
            own = strip(mid, kind, half)
            if 0 <= j < 4:
                return turn(own, base - 4 * j)
            if j == -1:
                return jnp.where(first, turn(strip(before, kind, half), base + 1), turn(own, base - 11))
            if j == -2:
                return jnp.where(first, turn(strip(before, kind, half), base - 11), turn(own, base - 7))
            if j == 4:
                return jnp.where(last, turn(strip(after, kind, half), base + 3), turn(own, base - 1))
            return jnp.where(last, turn(strip(after, kind, half), base - 1), turn(own, base - 5))

        for i in range(4):
            line = widened(i)
            emit(i, half, [line[j] for j in cols])
            if i == 0:
                emit(4, half, [
                    jnp.where(bottom, beyond(TOP, S, SW, SE, 12, j), turn(line[j], -4)) for j in cols
                ])
            if i == 1 and width == 2 and half == 0:
                emit(5, half, [
                    jnp.where(bottom, beyond(ROWS2, S, SW, SE, 12, j), turn(line[j], -4)) for j in cols
                ])
            if i == 2 and width == 2 and half == 1:
                emit(-2, half, [
                    jnp.where(top, beyond(ROWS2, N, NW, NE, 0, j), turn(line[j], 4)) for j in cols
                ])
            if i == 3:
                emit(-1, half, [
                    jnp.where(top, beyond(BOTTOM, N, NW, NE, 0, j), turn(line[j], 4)) for j in cols
                ])


def emit_odd(store, width, side):
    def emit(row, half, slabs):
        low = iota((16, 128), 1) < 64
        i = row + width - (1 - half)
        if 0 <= i < side:
            for j in range(side):
                store(i, j, half, jnp.where(low, slabs[j + 1], slabs[j]))

    return emit


def body(
    n_depth, n_plane,
    act_any, pw_any, pb, dw_any, db, cnt, nbr, vm_any, out,
    act, pw, dw, vm, load_sem,
    sel, spreads, hid, msk, x_in, y1, y2, y3, branch, m1, m2, weights, dweights,
    pool0, pool1, rim, rim_in, rim_mask, full_in,
    ring_ss, ring_rs, sib_ss, sib_rs, rim_ss, rim_rs, full_ss, full_rs,
):
    n_z = n_plane // 2
    pools = (pool0, pool1)
    d = lax.axis_index("depth")
    p = lax.axis_index("plane")
    z, c = p // 2, p % 2

    def z_at(offset):
        return lax.rem(z + offset + n_z, n_z)

    def plane_id(offset, core):
        return z_at(offset) * 2 + core

    def depth_id(way):
        return lax.rem(d + (1 if way == 0 else n_depth - 1), n_depth)

    loads = [
        pltpu.make_async_copy(src, dst, load_sem.at[k])
        for k, (src, dst) in enumerate(((act_any, act), (vm_any, vm), (pw_any, pw), (dw_any, dw)))
    ]
    for load in loads:
        load.start()
    barrier = pltpu.get_barrier_semaphore()
    for target in (
        {"plane": plane_id(1, 1 - c)}, {"plane": plane_id(-1, 1 - c)}, {"plane": z * 2 + 1 - c},
        {"plane": plane_id(2, c)}, {"plane": plane_id(-2, c)},
        {"depth": depth_id(0)}, {"depth": depth_id(1)},
    ):
        pl.semaphore_signal(barrier, inc=1, device_id=target, device_id_type=MESH)

    def block_ref(g, owner, item):
        return pools[g].at[owner, pl.ds(6 * item, 7 if g == 0 and item == 1 else 6)]

    def core_at(dist):
        return 1 - c if dist % 2 else c

    def ring_copy(g, way, k, m, item, owner_at):
        sign = -1 if way == RIGHT else 1
        ref = block_ref(g, plane_id(sign * owner_at, core_at(owner_at)), item)
        return pltpu.make_async_remote_copy(
            src_ref=ref, dst_ref=ref, send_sem=ring_ss.at[g, way, k + m - 1, item],
            recv_sem=ring_rs.at[g, way, k + m - 1, item],
            device_id={"plane": plane_id(-sign * m, core_at(m))}, device_id_type=MESH,
        )

    def ring_out(g, way, k, m, item):
        return ring_copy(g, way, k, m, item, k)

    def ring_in(g, way, dist, item):
        return ring_copy(g, way, dist - 1, 1, item, dist)

    def sib_copy(g, way, dist, item, mine):
        core = core_at(dist) if mine else 1 - core_at(dist)
        owner = plane_id(-dist if way == RIGHT else dist, core)
        key = 0 if dist == 0 else way * 4 + dist
        ref = block_ref(g, owner, item)
        return pltpu.make_async_remote_copy(
            src_ref=ref, dst_ref=ref, send_sem=sib_ss.at[g, key, item], recv_sem=sib_rs.at[g, key, item],
            device_id={"plane": z * 2 + 1 - c}, device_id_type=MESH,
        )

    def leads(way):
        return 0 if way == RIGHT else 1

    def items(g, way, dist):
        got = (leads(way), 1 - leads(way))
        if dist == 4:
            got = got[:1]
        return got

    def onward(g, way, dist, item):
        got = []
        if dist == 2 and item in items(g, way, 4):
            got.append(ring_out(g, way, 2, 2, item))
        if dist < 3:
            got.append(ring_out(g, way, dist, 1, item))
        return got

    def launch(g, way, item):
        for copy in onward(g, way, 0, item):
            copy.start()

    def share(g, item):
        sib_copy(g, RIGHT, 0, item, True).start()

    def pass_on(g, *dists):
        order = sorted(
            (items(g, way, dist).index(item), dist, way, item)
            for dist in dists for way in (RIGHT, LEFT) for item in items(g, way, dist)
        )
        for _, dist, way, item in order:
            ring_in(g, way, dist, item).wait_recv()
            for copy in onward(g, way, dist, item):
                copy.start()
            sib_copy(g, way, dist, item, True).start()

    def everything(g):
        got = [(RIGHT, 0, item) for item in (0, 1)]
        return got + [(way, dist, item) for dist in range(1, 5) for way in (RIGHT, LEFT) for item in items(g, way, dist)]

    def collect(g):
        for way, dist, item in everything(g):
            sib_copy(g, way, dist, item, False).wait_recv()

    def settle(g):
        for way, dist, item in everything(g):
            sib_copy(g, way, dist, item, True).wait_send()
        for dist in range(3):
            for way in (RIGHT, LEFT):
                for item in items(g, way, max(dist, 1)):
                    for copy in onward(g, way, dist, item):
                        copy.wait_send()

    def rim_copy(blk, way, t):
        return pltpu.make_async_remote_copy(
            src_ref=rim.at[blk, t], dst_ref=rim_in.at[blk, way, t],
            send_sem=rim_ss.at[blk, way, t], recv_sem=rim_rs.at[blk, way, t],
            device_id={"depth": depth_id(way)}, device_id_type=MESH,
        )

    def full_copy(blk, way, t):
        return pltpu.make_async_remote_copy(
            src_ref=branch.at[blk, t], dst_ref=full_in.at[blk, way, t],
            send_sem=full_ss.at[blk, way, t], recv_sem=full_rs.at[blk, way, t],
            device_id={"depth": depth_id(way)}, device_id_type=MESH,
        )

    r = iota((512, 1), 0)
    q, i, j, a, b = r // 128, (r // 32) % 4, (r // 8) % 4, (r // 4) % 2, r % 4
    cell = a * 256 + i * 64 + (q // 2) * 32 + b * 8 + j * 2 + q % 2
    sel[...] = jnp.where(cell == iota((512, 512), 1), 1.0, 0.0).astype(BF16)

    low128 = iota((128, 128), 1) < 64
    low16 = iota((16, 128), 1) < 64
    low64 = iota((64, 128), 1) < 64

    def to_patches(src, dst, live):
        for h in range(2):
            v = dot(sel[...], src[:, h * 512 : (h + 1) * 512], 1, 1)
            v = jnp.where(live > slot, v, 0.0)
            for half in range(2):
                even, odd = (v[(2 * half + k) * 128 : (2 * half + k + 1) * 128] for k in range(2))
                lanes = slice(half * 128, half * 128 + 128)
                rows = slice(h * 8, h * 8 + 8)
                dst[0, :, rows, lanes] = jnp.where(low128, even, pltpu.roll(odd, 64, 1)).reshape(16, 8, 128)
                dst[1, :, rows, lanes] = jnp.where(low128, pltpu.roll(even, 64, 1), odd).reshape(16, 8, 128)

    slot = iota((1, 128), 1) // 64
    loads[0].wait()
    to_patches(act[...], hid, cnt[p])

    def half_of(half):
        return slice(half * 128, half * 128 + 128)

    def slab_of(ref, t):
        return lambda i, j, half: ref[t, 4 * i + j, :, half_of(half)]

    for t in range(2):
        for (kind, half), value in strip_halves(slab_of(hid, t), True).items():
            pool0[p, 6 * t + kind, :, half_of(half)] = value.astype(BF16)

    loads[1].wait()
    spread = jnp.concatenate(
        [jnp.broadcast_to(vm[t].astype(F32), (64, 1024)) for t in range(2)], axis=0
    ).astype(BF16)
    to_patches(spread, msk, 2)
    lane64 = iota((16, 128), 1) % 64
    mask_out = jnp.zeros((16, 128), F32)
    for t in range(2):
        strips = strip_halves(slab_of(msk, t), True)
        for (kind, half), value in strips.items():
            rim_mask[t, kind, :, half_of(half)] = value
            if kind in (TOP, BOTTOM, FIRST, LAST):
                order = (TOP, BOTTOM, FIRST, LAST).index(kind)
                mask_out = jnp.where(lane64 == half * 8 + t * 4 + order, value, mask_out)
    pool0[p, MASK] = jnp.concatenate([mask_out, jnp.zeros((16, 128), F32)], axis=1).astype(BF16)

    pl.semaphore_wait(barrier, 7)
    for item in range(2):
        launch(0, RIGHT, item)
        launch(0, LEFT, 1 - item)
    share(0, 0)
    share(0, 1)

    def twice(w):
        unit = jnp.where(iota((64, 128), 0) == iota((64, 128), 1) % 64, 1.0, 0.0).astype(BF16)
        return dot(w, unit, 0, 0)

    def plane_weights(blk, layer):
        w = twice(pw[blk, layer])
        mirror_in, mirror_out = layer != 1, layer == 1
        for s in range(4):
            for q in range(4):
                u = 2 * (s // 2) + (1 - q // 2 if mirror_in else q // 2)
                v = 2 * (s % 2) + (1 - q % 2 if mirror_in else q % 2)
                rows = slice((s * 4 + q) * 64, (s * 4 + q + 1) * 64)
                for half in range(2):
                    parts = []
                    for col in range(2):
                        dr = u - (1 - half if mirror_out else half)
                        dc = v - (1 - col if mirror_out else col)
                        ok = 0 <= dr < 3 and 0 <= dc < 3
                        tap = dr * 3 + dc
                        parts.append(w[tap * 64 : (tap + 1) * 64] if ok else jnp.zeros((64, 128), F32))
                    weights[blk * 3 + layer, rows, half_of(half)] = jnp.where(low64, *parts).astype(BF16)

    def depth_weights(blk):
        w = twice(dw[blk])
        zero = jnp.zeros((64, 128), F32)
        for tap in range(3):
            part = w[tap * 64 : (tap + 1) * 64]
            if tap == 0:
                part = jnp.where(d > 0, part, 0.0)
            if tap == 2:
                part = jnp.where(d < n_depth - 1, part, 0.0)
            for q in range(4):
                rows = slice(tap * 256 + q * 64, tap * 256 + (q + 1) * 64)
                mine = jnp.where(low64, part, 0.0) if q % 2 == 0 else jnp.where(low64, 0.0, part)
                for half in range(2):
                    dweights[blk, rows, half_of(half)] = (mine if q // 2 == half else zero).astype(BF16)

    def four(v):
        two = jnp.concatenate([v, v], axis=1)
        return jnp.concatenate([two, two], axis=1)

    loads[2].wait()
    loads[3].wait()
    for blk in range(2):
        for layer in range(3):
            plane_weights(blk, layer)
        depth_weights(blk)
    m, n = iota((128, 256), 0), iota((128, 256), 1)
    for order in range(4):
        hit = (m // 64 == (n % 128) // 64) & ((m % 64) // 8 == n // 128) & (m % 4 == order)
        spreads[order] = jnp.where(hit, 1.0, 0.0).astype(BF16)
    pass_on(0, 1)
    pass_on(0, 2)
    pass_on(0, 3, 4)
    collect(0)

    group = {NW: BOTTOM, N: BOTTOM, NE: BOTTOM, W: LAST, E: FIRST, SW: TOP, S: TOP, SE: TOP}

    def around_mask(t, carry):
        spot = iota((16, 128), 1) % 64
        found = {}
        for kind in (TOP, BOTTOM, FIRST, LAST):
            order = (TOP, BOTTOM, FIRST, LAST).index(kind)
            ways = [k for k in range(8) if group[k] == kind]
            rows = []
            for k in ways:
                other = nbr[t, k]
                at = jnp.maximum(other, 0)
                keep = (spot % 8) // 4 == jnp.where(other >= 0, at % 2, 2)
                rows.append(jnp.where(keep, pool0[at // 2, MASK, :, :128].astype(F32), 0.0))
            wide = dot(jnp.concatenate(rows, axis=0).astype(BF16), spreads[order])
            for at, k in enumerate(ways):
                found[k] = wide[at * 16 : at * 16 + 16]

        def store_odd(i, j, half, value):
            m2[t, i, j, :, half_of(half)] = value

        odd = emit_odd(store_odd, 1, 5)

        def emit(row, half, slabs):
            for j in range(6):
                m1[t, row + 1, j, :, half_of(half)] = slabs[j]
            odd(row, half, slabs)

        surround(slab_of(msk, t), lambda k, kind, half: found[k][:, half_of(half)], 1, emit)
        return carry

    lax.fori_loop(0, 2, around_mask, 0)

    def conv(blk, layer, src, side, mask, dst):
        n = side - 1
        w = weights.at[blk * 3 + layer]
        for lo, hi in ((0, (n + 1) // 2), ((n + 1) // 2, n)):
            rows = (hi - lo) * n * 16
            total = four(pb[layer, blk : blk + 1, :])
            for s in range(4):
                si, sj = s // 2, s % 2
                tap = src[lo + si : hi + si, sj : sj + n].reshape(rows, 256)
                total = total + dot(tap, w[256 * s : 256 * s + 256])
            gated = total * (0.5 + 0.5 * jnp.tanh(0.5 * total)) * mask(lo, hi).reshape(rows, 256)
            dst[lo:hi] = gated.astype(BF16).reshape(hi - lo, n, 16, 256)

    def plane_layers(blk, tile, halo, last):
        def store_odd(i, j, half, value):
            x_in[i, j, :, half_of(half)] = value.astype(BF16)

        def strip(k, kind, half):
            if not halo:
                return jnp.zeros((16, 128), F32)
            other = nbr[tile, k]
            at = jnp.maximum(other, 0)
            value = pools[blk][at // 2, at % 2 * 6 + kind, :, half_of(half)].astype(F32)
            return jnp.where(other >= 0, value, 0.0)

        surround(slab_of(hid, tile), strip, 2, emit_odd(store_odd, 2, 7))
        conv(blk, 0, x_in, 7, lambda lo, hi: m1[tile, lo:hi], y1)
        conv(blk, 1, y1, 6, lambda lo, hi: m2[tile, lo:hi], y2)
        conv(blk, 2, y2, 5, lambda lo, hi: msk[tile, 4 * lo : 4 * hi], last)

    def send_rim(blk, tile, last):
        slab = lambda i, j, half: last[i, j, :, half_of(half)].astype(F32)
        for (kind, half), value in strip_halves(slab, True).items():
            rim[blk, tile, kind, :, half_of(half)] = value.astype(BF16)
        for way in range(2):
            rim_copy(blk, way, tile).start()

    def first_block(tile, carry):
        plane_layers(0, tile, True, branch.at[0, tile])
        send_rim(0, tile, branch.at[0, tile])
        return carry

    def early_block(tile, carry):
        plane_layers(1, tile, False, branch.at[1, tile])
        for way in range(2):
            full_copy(1, way, tile).start()
        return carry

    def second_block(tile, carry):
        plane_layers(1, tile, True, y3)
        send_rim(1, tile, y3)
        return carry

    def along_depth(blk, below, own, above):
        return dot(jnp.concatenate([below, own, above], axis=1), dweights[blk]) + four(db[blk : blk + 1, :])

    def residual(blk, t):
        for way in range(2):
            full_copy(blk, way, t).wait_recv()
        total = along_depth(
            blk, full_in[blk, 0, t].reshape(256, 256), branch[blk, t].reshape(256, 256),
            full_in[blk, 1, t].reshape(256, 256),
        )
        new = hid[t].reshape(256, 256) + msk[t].reshape(256, 256) * total
        hid[t] = new.astype(BF16).astype(F32).reshape(16, 16, 256)

    def rim_residual(blk, t):
        for way in range(2):
            rim_copy(blk, way, t).wait_recv()
        total = along_depth(
            blk, rim_in[blk, 0, t].reshape(96, 256), rim[blk, t].reshape(96, 256), rim_in[blk, 1, t].reshape(96, 256)
        )
        old = pools[blk][p, 6 * t : 6 * t + 6].astype(F32).reshape(96, 256)
        return (old + rim_mask[t].reshape(96, 256) * total).astype(BF16).reshape(6, 16, 256)

    def put_rim(t, strips):
        row = iota((16, 1), 0)
        first, last, top, bottom = row % 4 == 0, row % 4 == 3, row < 4, row >= 12
        high16 = iota((16, 128), 1) >= 64
        for half in range(2):
            kinds = [strips[kind, :, half_of(half)].astype(F32) for kind in range(6)]
            for i in range(4):
                for j in range(4):
                    value = new = hid[t, 4 * i + j, :, half_of(half)]
                    if j == 0:
                        new = jnp.where(first, turn(kinds[FIRST], -i), new)
                    if j == 3:
                        new = jnp.where(last, turn(kinds[LAST], 3 - i), new)
                    if j == 1:
                        new = jnp.where(first, jnp.where(high16, value, turn(kinds[COLS2], -i)), new)
                    if j == 2:
                        new = jnp.where(last, jnp.where(high16, turn(kinds[COLS2], 3 - i), value), new)
                    if i == 0 or (i == 1 and half == 0):
                        new = jnp.where(top, turn(kinds[TOP if i == 0 else ROWS2], -4 * j), new)
                    if i == 3 or (i == 2 and half == 1):
                        new = jnp.where(bottom, turn(kinds[BOTTOM if i == 3 else ROWS2], 12 - 4 * j), new)
                    if new is not value:
                        hid[t, 4 * i + j, :, half_of(half)] = new

    lax.fori_loop(0, 2, first_block, 0)
    for t in range(2):
        for way in range(2):
            full_copy(0, way, t).start()
    for t in range(2):
        pool1[p, 6 * t : 6 * t + 6] = rim_residual(0, t)
        launch(1, RIGHT if t == 0 else LEFT, t)
    launch(1, RIGHT, 1)
    launch(1, LEFT, 0)
    share(1, 0)
    share(1, 1)
    pass_on(1, 1)
    pass_on(1, 2)
    for t in range(2):
        residual(0, t)
    lax.fori_loop(0, 2, early_block, 0)
    pass_on(1, 3, 4)
    collect(1)
    lax.fori_loop(0, 2, second_block, 0)
    for t in range(2):
        residual(1, t)
    for t in range(2):
        put_rim(t, rim_residual(1, t))

    for h in range(2):
        parts = []
        for half in range(2):
            lanes, rows = half_of(half), slice(h * 8, h * 8 + 8)
            one = hid[0, :, rows, lanes].reshape(128, 128)
            two = hid[1, :, rows, lanes].reshape(128, 128)
            parts.append(jnp.where(low128, one, pltpu.roll(two, 64, 1)))
            parts.append(jnp.where(low128, pltpu.roll(one, 64, 1), two))
        back = dot(jnp.concatenate(parts, axis=0).astype(BF16), sel[...], 0, 0)
        out[:, h * 512 : (h + 1) * 512] = back.astype(BF16)

    settle(0)
    settle(1)
    for t in range(2):
        for way in range(2):
            for blk in range(2):
                rim_copy(blk, way, t).wait_send()
                full_copy(blk, way, t).wait_send()


def shards(mesh, activations, plane_weight, plane_bias, depth_weight, depth_bias, counts, neighbours, voxel_mask):
    n_depth, n_plane = mesh.shape["depth"], mesh.shape["plane"]
    vmem = pl.BlockSpec(memory_space=pltpu.VMEM)
    smem = pl.BlockSpec(memory_space=pltpu.SMEM)
    hbm = pl.BlockSpec(memory_space=pl.ANY)
    dma = pltpu.SemaphoreType.DMA
    out = pl.pallas_call(
        functools.partial(body, n_depth, n_plane),
        out_shape=jax.ShapeDtypeStruct((128, 1024), BF16),
        in_specs=[hbm, hbm, vmem, hbm, vmem, smem, smem, hbm],
        out_specs=vmem,
        scratch_shapes=[
            pltpu.VMEM((128, 1024), BF16),
            pltpu.VMEM(plane_weight.shape, BF16),
            pltpu.VMEM(depth_weight.shape, BF16),
            pltpu.VMEM((2, 1, 1024), jnp.int32),
            dma((4,)),
            pltpu.VMEM((512, 512), BF16),
            pltpu.VMEM((4, 128, 256), BF16),
            pltpu.VMEM((2, 16, 16, 256), F32),
            pltpu.VMEM((2, 16, 16, 256), F32),
            pltpu.VMEM((7, 7, 16, 256), BF16),
            pltpu.VMEM((6, 6, 16, 256), BF16),
            pltpu.VMEM((5, 5, 16, 256), BF16),
            pltpu.VMEM((4, 4, 16, 256), BF16),
            pltpu.VMEM((2, 2, 4, 4, 16, 256), BF16),
            pltpu.VMEM((2, 6, 6, 16, 256), F32),
            pltpu.VMEM((2, 5, 5, 16, 256), F32),
            pltpu.VMEM((6, 1024, 256), BF16),
            pltpu.VMEM((2, 768, 256), BF16),
            pltpu.VMEM((n_plane, 13, 16, 256), BF16),
            pltpu.VMEM((n_plane, 12, 16, 256), BF16),
            pltpu.VMEM((2, 2, 6, 16, 256), BF16),
            pltpu.VMEM((2, 2, 2, 6, 16, 256), BF16),
            pltpu.VMEM((2, 6, 16, 256), F32),
            pltpu.VMEM((2, 2, 2, 4, 4, 16, 256), BF16),
            dma((2, 2, 4, 2)),
            dma((2, 2, 4, 2)),
            dma((2, 9, 2)),
            dma((2, 9, 2)),
            dma((2, 2, 2)),
            dma((2, 2, 2)),
            dma((2, 2, 2)),
            dma((2, 2, 2)),
        ],
        compiler_params=pltpu.CompilerParams(
            collective_id=0, has_side_effects=True, vmem_limit_bytes=56 * 2**20
        ),
    )(
        activations.reshape(128, 1024), plane_weight, plane_bias.transpose(1, 0, 2), depth_weight, depth_bias, counts, neighbours,
        voxel_mask,
    )
    return out.reshape(activations.shape)


def solution(mesh):
    in_specs = (
        P("plane", "depth", None, None),
        P(),
        P(),
        P(),
        P(),
        P(),
        P("plane", None),
        P("plane", "depth", None),
    )
    out_specs = P("plane", "depth", None, None)
    return jax.shard_map(
        functools.partial(shards, mesh), mesh=mesh, in_specs=in_specs, out_specs=out_specs, check_vma=False
    )
```

```python
import functools

import jax
import jax.numpy as jnp
from jax import lax
from jax.experimental import pallas as pl
from jax.experimental.pallas import tpu as pltpu
from jax.sharding import PartitionSpec as P


F32, BF16 = jnp.float32, jnp.bfloat16
MESH = pl.DeviceIdType.MESH
RIGHT, LEFT = 0, 1
MASK = 12
NW, N, NE, W, E, SW, S, SE = range(8)
TOP, BOTTOM, ROWS2, FIRST, LAST, COLS2 = range(6)


def iota(shape, dim):
    return lax.broadcasted_iota(jnp.int32, shape, dim)


def turn(x, k):
    k %= 16
    return pltpu.roll(x, k, 0) if k else x


def dot(a, b, ca=1, cb=0):
    return lax.dot_general(a, b, (((ca,), (cb,)), ((), ())), preferred_element_type=F32)


def row_strip(slab, a):
    row = iota((16, 1), 0)
    out = turn(slab(0), -4 * a)
    for j in range(1, 4):
        out = jnp.where(row // 4 == j, turn(slab(j), 4 * j - 4 * a), out)
    return out


def col_strip(slab, b):
    row = iota((16, 1), 0)
    out = turn(slab(0), -b)
    for i in range(1, 4):
        out = jnp.where(row % 4 == i, turn(slab(i), i - b), out)
    return out


def strip_halves(slab, wide):
    low = iota((16, 128), 1) < 64
    out = {}
    for half in range(2):
        out[TOP, half] = row_strip(lambda j: slab(0, j, half), 0)
        out[BOTTOM, half] = row_strip(lambda j: slab(3, j, half), 3)
        out[FIRST, half] = col_strip(lambda i: slab(i, 0, half), 0)
        out[LAST, half] = col_strip(lambda i: slab(i, 3, half), 3)
        if wide:
            if half == 0:
                out[ROWS2, half] = row_strip(lambda j: slab(1, j, half), 0)
            else:
                out[ROWS2, half] = row_strip(lambda j: slab(2, j, half), 3)
            out[COLS2, half] = jnp.where(
                low, col_strip(lambda i: slab(i, 1, half), 0), col_strip(lambda i: slab(i, 2, half), 3)
            )
    return out


def surround(slab, strip, width, emit):
    row = iota((16, 1), 0)
    first, last = row % 4 == 0, row % 4 == 3
    top, bottom = row < 4, row >= 12
    cols = range(-width, 4 + width)
    for half in range(2):

        def widened(i):
            out = {j: slab(i, j, half) for j in range(4)}
            for j in cols:
                if j == -1:
                    out[j] = jnp.where(first, turn(strip(W, LAST, half), -i), turn(slab(i, 3, half), 1))
                if j == -2:
                    out[j] = jnp.where(first, turn(strip(W, COLS2, half), -i), turn(slab(i, 2, half), 1))
                if j == 4:
                    out[j] = jnp.where(last, turn(strip(E, FIRST, half), 3 - i), turn(slab(i, 0, half), -1))
                if j == 5:
                    out[j] = jnp.where(last, turn(strip(E, COLS2, half), 3 - i), turn(slab(i, 1, half), -1))
            return out

        def beyond(kind, mid, before, after, base, j):
            own = strip(mid, kind, half)
            if 0 <= j < 4:
                return turn(own, base - 4 * j)
            if j == -1:
                return jnp.where(first, turn(strip(before, kind, half), base + 1), turn(own, base - 11))
            if j == -2:
                return jnp.where(first, turn(strip(before, kind, half), base - 11), turn(own, base - 7))
            if j == 4:
                return jnp.where(last, turn(strip(after, kind, half), base + 3), turn(own, base - 1))
            return jnp.where(last, turn(strip(after, kind, half), base - 1), turn(own, base - 5))

        for i in range(4):
            line = widened(i)
            emit(i, half, [line[j] for j in cols])
            if i == 0:
                emit(4, half, [
                    jnp.where(bottom, beyond(TOP, S, SW, SE, 12, j), turn(line[j], -4)) for j in cols
                ])
            if i == 1 and width == 2 and half == 0:
                emit(5, half, [
                    jnp.where(bottom, beyond(ROWS2, S, SW, SE, 12, j), turn(line[j], -4)) for j in cols
                ])
            if i == 2 and width == 2 and half == 1:
                emit(-2, half, [
                    jnp.where(top, beyond(ROWS2, N, NW, NE, 0, j), turn(line[j], 4)) for j in cols
                ])
            if i == 3:
                emit(-1, half, [
                    jnp.where(top, beyond(BOTTOM, N, NW, NE, 0, j), turn(line[j], 4)) for j in cols
                ])


def emit_odd(store, width, side):
    def emit(row, half, slabs):
        low = iota((16, 128), 1) < 64
        i = row + width - (1 - half)
        if 0 <= i < side:
            for j in range(side):
                store(i, j, half, jnp.where(low, slabs[j + 1], slabs[j]))

    return emit


def body(
    n_depth, n_plane,
    act_any, pw_any, pb, dw_any, db, cnt, nbr, vm_any, out,
    act, pw, dw, vm, load_sem,
    sel, spreads, hid, msk, x_in, y1, y2, y3, branch, m1, m2, weights, dweights,
    pool0, pool1, rim, rim_in, rim_mask, full_in,
    ring_ss, ring_rs, sib_ss, sib_rs, rim_ss, rim_rs, full_ss, full_rs,
):
    n_z = n_plane // 2
    pools = (pool0, pool1)
    d = lax.axis_index("depth")
    p = lax.axis_index("plane")
    z, c = p // 2, p % 2

    def z_at(offset):
        return lax.rem(z + offset + n_z, n_z)

    def plane_id(offset, core):
        return z_at(offset) * 2 + core

    def depth_id(way):
        return lax.rem(d + (1 if way == 0 else n_depth - 1), n_depth)

    loads = [
        pltpu.make_async_copy(src, dst, load_sem.at[k])
        for k, (src, dst) in enumerate(((act_any, act), (vm_any, vm), (pw_any, pw), (dw_any, dw)))
    ]
    for load in loads:
        load.start()
    barrier = pltpu.get_barrier_semaphore()
    for target in (
        {"plane": plane_id(1, 1 - c)}, {"plane": plane_id(-1, 1 - c)}, {"plane": z * 2 + 1 - c},
        {"plane": plane_id(2, c)}, {"plane": plane_id(-2, c)},
        {"depth": depth_id(0)}, {"depth": depth_id(1)},
    ):
        pl.semaphore_signal(barrier, inc=1, device_id=target, device_id_type=MESH)

    def block_ref(g, owner, item):
        return pools[g].at[owner, pl.ds(6 * item, 7 if g == 0 and item == 1 else 6)]

    def core_at(dist):
        return 1 - c if dist % 2 else c

    def ring_copy(g, way, k, m, item, owner_at):
        sign = -1 if way == RIGHT else 1
        ref = block_ref(g, plane_id(sign * owner_at, core_at(owner_at)), item)
        return pltpu.make_async_remote_copy(
            src_ref=ref, dst_ref=ref, send_sem=ring_ss.at[g, way, k + m - 1, item],
            recv_sem=ring_rs.at[g, way, k + m - 1, item],
            device_id={"plane": plane_id(-sign * m, core_at(m))}, device_id_type=MESH,
        )

    def ring_out(g, way, k, m, item):
        return ring_copy(g, way, k, m, item, k)

    def ring_in(g, way, dist, item):
        return ring_copy(g, way, dist - 1, 1, item, dist)

    def sib_copy(g, way, dist, item, mine):
        core = core_at(dist) if mine else 1 - core_at(dist)
        owner = plane_id(-dist if way == RIGHT else dist, core)
        key = 0 if dist == 0 else way * 4 + dist
        ref = block_ref(g, owner, item)
        return pltpu.make_async_remote_copy(
            src_ref=ref, dst_ref=ref, send_sem=sib_ss.at[g, key, item], recv_sem=sib_rs.at[g, key, item],
            device_id={"plane": z * 2 + 1 - c}, device_id_type=MESH,
        )

    def leads(way):
        return 0 if way == RIGHT else 1

    def items(g, way, dist):
        got = (leads(way), 1 - leads(way))
        if dist == 4:
            got = got[:1]
        return got

    def onward(g, way, dist, item):
        got = []
        if dist == 2 and item in items(g, way, 4):
            got.append(ring_out(g, way, 2, 2, item))
        if dist < 3:
            got.append(ring_out(g, way, dist, 1, item))
        return got

    def launch(g, way, item):
        for copy in onward(g, way, 0, item):
            copy.start()

    def share(g, item):
        sib_copy(g, RIGHT, 0, item, True).start()

    def pass_on(g, *dists):
        order = sorted(
            (items(g, way, dist).index(item), dist, way, item)
            for dist in dists for way in (RIGHT, LEFT) for item in items(g, way, dist)
        )
        for _, dist, way, item in order:
            ring_in(g, way, dist, item).wait_recv()
            for copy in onward(g, way, dist, item):
                copy.start()
            sib_copy(g, way, dist, item, True).start()

    def everything(g):
        got = [(RIGHT, 0, item) for item in (0, 1)]
        return got + [(way, dist, item) for dist in range(1, 5) for way in (RIGHT, LEFT) for item in items(g, way, dist)]

    def collect(g):
        for way, dist, item in everything(g):
            sib_copy(g, way, dist, item, False).wait_recv()

    def settle(g):
        for way, dist, item in everything(g):
            sib_copy(g, way, dist, item, True).wait_send()
        for dist in range(3):
            for way in (RIGHT, LEFT):
                for item in items(g, way, max(dist, 1)):
                    for copy in onward(g, way, dist, item):
                        copy.wait_send()

    def rim_copy(blk, way, t):
        return pltpu.make_async_remote_copy(
            src_ref=rim.at[blk, t], dst_ref=rim_in.at[blk, way, t],
            send_sem=rim_ss.at[blk, way, t], recv_sem=rim_rs.at[blk, way, t],
            device_id={"depth": depth_id(way)}, device_id_type=MESH,
        )

    def full_copy(blk, way, t):
        return pltpu.make_async_remote_copy(
            src_ref=branch.at[blk, t], dst_ref=full_in.at[blk, way, t],
            send_sem=full_ss.at[blk, way, t], recv_sem=full_rs.at[blk, way, t],
            device_id={"depth": depth_id(way)}, device_id_type=MESH,
        )

    r = iota((512, 1), 0)
    q, i, j, a, b = r // 128, (r // 32) % 4, (r // 8) % 4, (r // 4) % 2, r % 4
    cell = a * 256 + i * 64 + (q // 2) * 32 + b * 8 + j * 2 + q % 2
    sel[...] = jnp.where(cell == iota((512, 512), 1), 1.0, 0.0).astype(BF16)

    low128 = iota((128, 128), 1) < 64
    low16 = iota((16, 128), 1) < 64
    low64 = iota((64, 128), 1) < 64

    def to_patches(src, dst, live):
        for h in range(2):
            v = dot(sel[...], src[:, h * 512 : (h + 1) * 512], 1, 1)
            v = jnp.where(live > slot, v, 0.0)
            for half in range(2):
                even, odd = (v[(2 * half + k) * 128 : (2 * half + k + 1) * 128] for k in range(2))
                lanes = slice(half * 128, half * 128 + 128)
                rows = slice(h * 8, h * 8 + 8)
                dst[0, :, rows, lanes] = jnp.where(low128, even, pltpu.roll(odd, 64, 1)).reshape(16, 8, 128)
                dst[1, :, rows, lanes] = jnp.where(low128, pltpu.roll(even, 64, 1), odd).reshape(16, 8, 128)

    slot = iota((1, 128), 1) // 64
    loads[0].wait()
    to_patches(act[...], hid, cnt[p])

    def half_of(half):
        return slice(half * 128, half * 128 + 128)

    def slab_of(ref, t):
        return lambda i, j, half: ref[t, 4 * i + j, :, half_of(half)]

    for t in range(2):
        for (kind, half), value in strip_halves(slab_of(hid, t), True).items():
            pool0[p, 6 * t + kind, :, half_of(half)] = value.astype(BF16)

    loads[1].wait()
    spread = jnp.concatenate(
        [jnp.broadcast_to(vm[t].astype(F32), (64, 1024)) for t in range(2)], axis=0
    ).astype(BF16)
    to_patches(spread, msk, 2)
    lane64 = iota((16, 128), 1) % 64
    mask_out = jnp.zeros((16, 128), F32)
    for t in range(2):
        strips = strip_halves(slab_of(msk, t), True)
        for (kind, half), value in strips.items():
            rim_mask[t, kind, :, half_of(half)] = value
            if kind in (TOP, BOTTOM, FIRST, LAST):
                order = (TOP, BOTTOM, FIRST, LAST).index(kind)
                mask_out = jnp.where(lane64 == half * 8 + t * 4 + order, value, mask_out)
    pool0[p, MASK] = jnp.concatenate([mask_out, jnp.zeros((16, 128), F32)], axis=1).astype(BF16)

    pl.semaphore_wait(barrier, 7)
    for item in range(2):
        launch(0, RIGHT, item)
        launch(0, LEFT, 1 - item)
    share(0, 0)
    share(0, 1)

    def twice(w, scale):
        unit = jnp.where(iota((64, 128), 0) == iota((64, 128), 1) % 64, scale, 0.0).astype(BF16)
        return dot(w, unit, 0, 0)

    def plane_weights(blk, layer):
        w = twice(pw[blk, layer], 0.5)
        mirror_in, mirror_out = layer != 1, layer == 1
        for s in range(4):
            for q in range(4):
                u = 2 * (s // 2) + (1 - q // 2 if mirror_in else q // 2)
                v = 2 * (s % 2) + (1 - q % 2 if mirror_in else q % 2)
                rows = slice((s * 4 + q) * 64, (s * 4 + q + 1) * 64)
                for half in range(2):
                    parts = []
                    for col in range(2):
                        dr = u - (1 - half if mirror_out else half)
                        dc = v - (1 - col if mirror_out else col)
                        ok = 0 <= dr < 3 and 0 <= dc < 3
                        tap = dr * 3 + dc
                        parts.append(w[tap * 64 : (tap + 1) * 64] if ok else jnp.zeros((64, 128), F32))
                    weights[blk * 3 + layer, rows, half_of(half)] = jnp.where(low64, *parts).astype(BF16)

    def depth_weights(blk):
        w = twice(dw[blk], 1.0)
        zero = jnp.zeros((64, 128), F32)
        for tap in range(3):
            part = w[tap * 64 : (tap + 1) * 64]
            if tap == 0:
                part = jnp.where(d > 0, part, 0.0)
            if tap == 2:
                part = jnp.where(d < n_depth - 1, part, 0.0)
            for q in range(4):
                rows = slice(tap * 256 + q * 64, tap * 256 + (q + 1) * 64)
                mine = jnp.where(low64, part, 0.0) if q % 2 == 0 else jnp.where(low64, 0.0, part)
                for half in range(2):
                    dweights[blk, rows, half_of(half)] = (mine if q // 2 == half else zero).astype(BF16)

    def four(v):
        two = jnp.concatenate([v, v], axis=1)
        return jnp.concatenate([two, two], axis=1)

    loads[2].wait()
    loads[3].wait()
    for blk in range(2):
        for layer in range(3):
            plane_weights(blk, layer)
        depth_weights(blk)
    m, n = iota((128, 256), 0), iota((128, 256), 1)
    for order in range(4):
        hit = (m // 64 == (n % 128) // 64) & ((m % 64) // 8 == n // 128) & (m % 4 == order)
        spreads[order] = jnp.where(hit, 1.0, 0.0).astype(BF16)
    pass_on(0, 1)
    pass_on(0, 2)
    pass_on(0, 3, 4)
    collect(0)

    group = {NW: BOTTOM, N: BOTTOM, NE: BOTTOM, W: LAST, E: FIRST, SW: TOP, S: TOP, SE: TOP}

    def around_mask(t, carry):
        spot = iota((16, 128), 1) % 64
        found = {}
        for kind in (TOP, BOTTOM, FIRST, LAST):
            order = (TOP, BOTTOM, FIRST, LAST).index(kind)
            ways = [k for k in range(8) if group[k] == kind]
            rows = []
            for k in ways:
                other = nbr[t, k]
                at = jnp.maximum(other, 0)
                keep = (spot % 8) // 4 == jnp.where(other >= 0, at % 2, 2)
                rows.append(jnp.where(keep, pool0[at // 2, MASK, :, :128].astype(F32), 0.0))
            wide = dot(jnp.concatenate(rows, axis=0).astype(BF16), spreads[order])
            for at, k in enumerate(ways):
                found[k] = wide[at * 16 : at * 16 + 16]

        def store_odd(i, j, half, value):
            m2[t, i, j, :, half_of(half)] = value

        odd = emit_odd(store_odd, 1, 5)

        def emit(row, half, slabs):
            for j in range(6):
                m1[t, row + 1, j, :, half_of(half)] = slabs[j]
            odd(row, half, slabs)

        surround(slab_of(msk, t), lambda k, kind, half: found[k][:, half_of(half)], 1, emit)
        return carry

    lax.fori_loop(0, 2, around_mask, 0)

    def conv(blk, layer, src, side, mask, dst):
        n = side - 1
        w = weights.at[blk * 3 + layer]
        for lo, hi in ((0, (n + 1) // 2), ((n + 1) // 2, n)):
            rows = (hi - lo) * n * 16
            half_sum = four(0.5 * pb[layer, blk : blk + 1, :])
            for s in range(4):
                si, sj = s // 2, s % 2
                tap = src[lo + si : hi + si, sj : sj + n].reshape(rows, 256)
                half_sum = half_sum + dot(tap, w[256 * s : 256 * s + 256])
            gated = (half_sum + half_sum * jnp.tanh(half_sum)) * mask(lo, hi).reshape(rows, 256)
            dst[lo:hi] = gated.astype(BF16).reshape(hi - lo, n, 16, 256)

    def plane_layers(blk, tile, halo, last):
        def store_odd(i, j, half, value):
            x_in[i, j, :, half_of(half)] = value.astype(BF16)

        def strip(k, kind, half):
            if not halo:
                return jnp.zeros((16, 128), F32)
            other = nbr[tile, k]
            at = jnp.maximum(other, 0)
            value = pools[blk][at // 2, at % 2 * 6 + kind, :, half_of(half)].astype(F32)
            return jnp.where(other >= 0, value, 0.0)

        surround(slab_of(hid, tile), strip, 2, emit_odd(store_odd, 2, 7))
        conv(blk, 0, x_in, 7, lambda lo, hi: m1[tile, lo:hi], y1)
        conv(blk, 1, y1, 6, lambda lo, hi: m2[tile, lo:hi], y2)
        conv(blk, 2, y2, 5, lambda lo, hi: msk[tile, 4 * lo : 4 * hi], last)

    def send_rim(blk, tile, last):
        slab = lambda i, j, half: last[i, j, :, half_of(half)].astype(F32)
        for (kind, half), value in strip_halves(slab, True).items():
            rim[blk, tile, kind, :, half_of(half)] = value.astype(BF16)
        for way in range(2):
            rim_copy(blk, way, tile).start()

    def first_block(tile, carry):
        plane_layers(0, tile, True, branch.at[0, tile])
        send_rim(0, tile, branch.at[0, tile])
        return carry

    def early_block(tile, carry):
        plane_layers(1, tile, False, branch.at[1, tile])
        for way in range(2):
            full_copy(1, way, tile).start()
        return carry

    def second_block(tile, carry):
        plane_layers(1, tile, True, y3)
        send_rim(1, tile, y3)
        return carry

    def along_depth(blk, below, own, above):
        return dot(jnp.concatenate([below, own, above], axis=1), dweights[blk]) + four(db[blk : blk + 1, :])

    def residual(blk, t):
        for way in range(2):
            full_copy(blk, way, t).wait_recv()
        total = along_depth(
            blk, full_in[blk, 0, t].reshape(256, 256), branch[blk, t].reshape(256, 256),
            full_in[blk, 1, t].reshape(256, 256),
        )
        new = hid[t].reshape(256, 256) + msk[t].reshape(256, 256) * total
        hid[t] = new.astype(BF16).astype(F32).reshape(16, 16, 256)

    def rim_residual(blk, t):
        for way in range(2):
            rim_copy(blk, way, t).wait_recv()
        total = along_depth(
            blk, rim_in[blk, 0, t].reshape(96, 256), rim[blk, t].reshape(96, 256), rim_in[blk, 1, t].reshape(96, 256)
        )
        old = pools[blk][p, 6 * t : 6 * t + 6].astype(F32).reshape(96, 256)
        return (old + rim_mask[t].reshape(96, 256) * total).astype(BF16).reshape(6, 16, 256)

    def put_rim(t, strips):
        row = iota((16, 1), 0)
        first, last, top, bottom = row % 4 == 0, row % 4 == 3, row < 4, row >= 12
        high16 = iota((16, 128), 1) >= 64
        for half in range(2):
            kinds = [strips[kind, :, half_of(half)].astype(F32) for kind in range(6)]
            for i in range(4):
                for j in range(4):
                    value = new = hid[t, 4 * i + j, :, half_of(half)]
                    if j == 0:
                        new = jnp.where(first, turn(kinds[FIRST], -i), new)
                    if j == 3:
                        new = jnp.where(last, turn(kinds[LAST], 3 - i), new)
                    if j == 1:
                        new = jnp.where(first, jnp.where(high16, value, turn(kinds[COLS2], -i)), new)
                    if j == 2:
                        new = jnp.where(last, jnp.where(high16, turn(kinds[COLS2], 3 - i), value), new)
                    if i == 0 or (i == 1 and half == 0):
                        new = jnp.where(top, turn(kinds[TOP if i == 0 else ROWS2], -4 * j), new)
                    if i == 3 or (i == 2 and half == 1):
                        new = jnp.where(bottom, turn(kinds[BOTTOM if i == 3 else ROWS2], 12 - 4 * j), new)
                    if new is not value:
                        hid[t, 4 * i + j, :, half_of(half)] = new

    lax.fori_loop(0, 2, first_block, 0)
    for t in range(2):
        for way in range(2):
            full_copy(0, way, t).start()
    for t in range(2):
        pool1[p, 6 * t : 6 * t + 6] = rim_residual(0, t)
        launch(1, RIGHT if t == 0 else LEFT, t)
    launch(1, RIGHT, 1)
    launch(1, LEFT, 0)
    share(1, 0)
    share(1, 1)
    pass_on(1, 1)
    pass_on(1, 2)
    for t in range(2):
        residual(0, t)
    lax.fori_loop(0, 2, early_block, 0)
    pass_on(1, 3, 4)
    collect(1)
    lax.fori_loop(0, 2, second_block, 0)
    for t in range(2):
        residual(1, t)
    for t in range(2):
        put_rim(t, rim_residual(1, t))

    for h in range(2):
        parts = []
        for half in range(2):
            lanes, rows = half_of(half), slice(h * 8, h * 8 + 8)
            one = hid[0, :, rows, lanes].reshape(128, 128)
            two = hid[1, :, rows, lanes].reshape(128, 128)
            parts.append(jnp.where(low128, one, pltpu.roll(two, 64, 1)))
            parts.append(jnp.where(low128, pltpu.roll(one, 64, 1), two))
        back = dot(jnp.concatenate(parts, axis=0).astype(BF16), sel[...], 0, 0)
        out[:, h * 512 : (h + 1) * 512] = back.astype(BF16)

    settle(0)
    settle(1)
    for t in range(2):
        for way in range(2):
            for blk in range(2):
                rim_copy(blk, way, t).wait_send()
                full_copy(blk, way, t).wait_send()


def shards(mesh, activations, plane_weight, plane_bias, depth_weight, depth_bias, counts, neighbours, voxel_mask):
    n_depth, n_plane = mesh.shape["depth"], mesh.shape["plane"]
    vmem = pl.BlockSpec(memory_space=pltpu.VMEM)
    smem = pl.BlockSpec(memory_space=pltpu.SMEM)
    hbm = pl.BlockSpec(memory_space=pl.ANY)
    dma = pltpu.SemaphoreType.DMA
    out = pl.pallas_call(
        functools.partial(body, n_depth, n_plane),
        out_shape=jax.ShapeDtypeStruct((128, 1024), BF16),
        in_specs=[hbm, hbm, vmem, hbm, vmem, smem, smem, hbm],
        out_specs=vmem,
        scratch_shapes=[
            pltpu.VMEM((128, 1024), BF16),
            pltpu.VMEM(plane_weight.shape, BF16),
            pltpu.VMEM(depth_weight.shape, BF16),
            pltpu.VMEM((2, 1, 1024), jnp.int32),
            dma((4,)),
            pltpu.VMEM((512, 512), BF16),
            pltpu.VMEM((4, 128, 256), BF16),
            pltpu.VMEM((2, 16, 16, 256), F32),
            pltpu.VMEM((2, 16, 16, 256), F32),
            pltpu.VMEM((7, 7, 16, 256), BF16),
            pltpu.VMEM((6, 6, 16, 256), BF16),
            pltpu.VMEM((5, 5, 16, 256), BF16),
            pltpu.VMEM((4, 4, 16, 256), BF16),
            pltpu.VMEM((2, 2, 4, 4, 16, 256), BF16),
            pltpu.VMEM((2, 6, 6, 16, 256), F32),
            pltpu.VMEM((2, 5, 5, 16, 256), F32),
            pltpu.VMEM((6, 1024, 256), BF16),
            pltpu.VMEM((2, 768, 256), BF16),
            pltpu.VMEM((n_plane, 13, 16, 256), BF16),
            pltpu.VMEM((n_plane, 12, 16, 256), BF16),
            pltpu.VMEM((2, 2, 6, 16, 256), BF16),
            pltpu.VMEM((2, 2, 2, 6, 16, 256), BF16),
            pltpu.VMEM((2, 6, 16, 256), F32),
            pltpu.VMEM((2, 2, 2, 4, 4, 16, 256), BF16),
            dma((2, 2, 4, 2)),
            dma((2, 2, 4, 2)),
            dma((2, 9, 2)),
            dma((2, 9, 2)),
            dma((2, 2, 2)),
            dma((2, 2, 2)),
            dma((2, 2, 2)),
            dma((2, 2, 2)),
        ],
        compiler_params=pltpu.CompilerParams(
            collective_id=0, has_side_effects=True, vmem_limit_bytes=56 * 2**20
        ),
    )(
        activations.reshape(128, 1024), plane_weight, plane_bias.transpose(1, 0, 2), depth_weight, depth_bias, counts, neighbours,
        voxel_mask,
    )
    return out.reshape(activations.shape)


def solution(mesh):
    in_specs = (
        P("plane", "depth", None, None),
        P(),
        P(),
        P(),
        P(),
        P(),
        P("plane", None),
        P("plane", "depth", None),
    )
    out_specs = P("plane", "depth", None, None)
    return jax.shard_map(
        functools.partial(shards, mesh), mesh=mesh, in_specs=in_specs, out_specs=out_specs, check_vma=False
    )
```
